512 devices in a mesh: dp: 16 (over y, x), seq: 32 (over z, core).
Axes of the slice: x: 4, y: 4, z: 16, core: 2. Of those that a mesh axis runs over, the one named last changes fastest.
Arguments:
- hidden: bfloat16 [16, 4096, 1280], P('dp', 'seq'), may hold values from -6 to 6
- gate_probs: float32 [16, 2, 4096], P('dp', None, 'seq'), may hold values from 0.05 to 0.95
- expert_ids: int32 [16, 2, 4096], P('dp', None, 'seq'), may hold values from 0 to 31, as said below
- slot_ids: int32 [16, 2, 4096], P('dp', None, 'seq'), may hold values from 0 to 2, as said below
- mask_pos: int32 [16, 2048], P('dp', 'seq'), may hold values from 0 to 127, as said below
- distractors: int32 [16, 10, 2048], P('dp', None, 'seq'), may hold values from 0 to 2047, as said below
- targets: bfloat16 [16, 2048, 1280], P('dp', 'seq'), may hold values from -6 to 6
- weight_in: bfloat16 [32, 1280, 5120], P('seq', None, 'dp'), may hold values from -0.15625 to 0.15625
- weight_out: bfloat16 [32, 5120, 1280], P('seq', 'dp'), may hold values from -0.078125 to 0.078125
Outputs:
- frame_loss: float32 [16, 2048], P('dp', 'seq')
- gate_grad: float32 [16, 2, 4096], P('dp', None, 'seq')
- grad_hidden: bfloat16 [16, 4096, 1280], P('dp', 'seq')
- grad_weight_in: bfloat16 [32, 1280, 5120], P('seq', None, 'dp')
- grad_weight_out: bfloat16 [32, 5120, 1280], P('seq', 'dp')
The draws below stay inside these ranges and needn't reach their ends.
Inputs may be any that keep to these rules, and one draw needn't show every extreme that they name: expert_ids[r, 0, f] and expert_ids[r, 1, f] differ. In each device's block of 128 frames every expert is the first choice of exactly 4 frames. slot_ids[r, k, f] is the number of assignments to the same expert that come earlier in the same block of 128 frames (frames in order, the first choice before the second), replaced by 2 when it reaches 2; 2 marks a dropped assignment. Each of the 2 slots of every expert is taken by exactly one assignment of every block. `mask_pos`: each device's 64 entries are distinct and rising. `distractors`: entry [r, j, i] indexes the masked frames of recording r and differs from i. Of the 640 entries of one device's masked frames, exactly 20 lie in each block of 64 masked frames.
All inputs are finite; a program needn't handle non-finite values.
Results may differ from the reference program's by a relative error of at most 0.008.
Values may be sent and summed in bfloat16 or wider, within the bound.
A program may use at most 64 MiB of HBM per device.

```python
import jax
import jax.numpy as jnp
from jax import lax

D = 1280
FF = 5120
TOP = 2
CAP = 2
NEG = 10
FR_DEV = 128
M_DEV = 64
EXPERTS = 32
RECS = 16
FRAMES = 4096
MASKED = 2048
N_DP = 16
N_SEQ = 32


def route_tables(key):
    block_count = RECS * (FRAMES // FR_DEV)
    expert_cycle = jnp.arange(FR_DEV, dtype=jnp.int32) % EXPERTS
    block_keys = jax.random.split(key, block_count)
    first_pick = jax.vmap(lambda block_key: jax.random.permutation(block_key, expert_cycle))(block_keys)
    offset = jax.random.randint(jax.random.fold_in(key, 7), (block_count, FR_DEV), 1, EXPERTS)
    second_pick = (first_pick + offset) % EXPERTS
    picks = jnp.stack([first_pick, second_pick], axis=2).astype(jnp.int32)
    flat_picks = picks.reshape(block_count, FR_DEV * TOP)
    onehot = (flat_picks[:, :, None] == jnp.arange(EXPERTS, dtype=jnp.int32)[None, None, :]).astype(jnp.int32)
    earlier = jnp.cumsum(onehot, axis=1) - onehot
    arrival = jnp.sum(earlier * onehot, axis=2)
    slot_cap = jnp.minimum(arrival, CAP).reshape(block_count, FR_DEV, TOP)

    def layout(array):
        shaped = array.reshape(RECS, FRAMES // FR_DEV, FR_DEV, TOP).transpose(0, 3, 1, 2)
        return shaped.reshape(RECS, TOP, FRAMES).astype(jnp.int32)
    return (layout(picks), layout(slot_cap))


def draw_expert_ids(key, part):
    return route_tables(key)[0]


def draw_slot_ids(key, part):
    return route_tables(key)[1]


def draw_mask_pos(key, part):
    key = jax.random.fold_in(key, 11)
    block_keys = jax.random.split(key, RECS * (FRAMES // FR_DEV))

    def choose(block_key):
        return jnp.sort(jax.random.permutation(block_key, FR_DEV)[:M_DEV])
    chosen = jax.vmap(choose)(block_keys)
    return chosen.reshape(RECS, MASKED).astype(jnp.int32)


def draw_distractors(key, part):
    key = jax.random.fold_in(key, 23)
    owners = MASKED // M_DEV
    block_count = RECS * owners
    per_owner = M_DEV * NEG // owners
    local_pick = jax.random.randint(key, (block_count, owners, per_owner), 0, M_DEV)
    owner_iota = jnp.arange(owners, dtype=jnp.int32)[None, :, None]
    wanted = (owner_iota * M_DEV + local_pick).reshape(block_count, M_DEV * NEG)
    block_keys = jax.random.split(jax.random.fold_in(key, 5), block_count)
    wanted = jax.vmap(lambda block_key, values: jax.random.permutation(block_key, values))(block_keys, wanted)
    wanted = wanted.reshape(RECS, owners, M_DEV, NEG)
    block_id = jnp.arange(owners, dtype=jnp.int32)[None, :, None, None]
    frame_iota = jnp.arange(M_DEV, dtype=jnp.int32)[None, None, :, None]
    self_id = block_id * M_DEV + frame_iota
    neighbor = block_id * M_DEV + (frame_iota + 1) % M_DEV
    wanted = jnp.where(wanted == self_id, neighbor, wanted)
    return wanted.transpose(0, 3, 1, 2).reshape(RECS, NEG, MASKED).astype(jnp.int32)


def steps_of(stream_key, extent, pieces, smallest, largest):
    level = 1.0
    for position, blocks in pieces:
        steps = jax.random.uniform(jax.random.fold_in(jax.random.fold_in(stream_key, 6), position), (blocks,), jnp.float32, smallest / len(pieces), largest / len(pieces))
        level = level * jnp.repeat(jnp.exp(steps), extent[position] // blocks).reshape((-1,) + (1,) * (len(extent) - 1 - position))
    return level


def scatter_about(rng, shape, scale, most, pieces=(), held_as=jnp.bfloat16):
    result = scale * jax.random.normal(rng, shape, jnp.float32)
    if pieces:
        result = result * steps_of(rng, shape, pieces, -0.22, 0.18)
    return jnp.clip(result, -most, most).astype(held_as)


def setup_inputs(seed: int = 0) -> dict:
    seeds = jax.random.split(jax.random.key(seed), 10)
    hidden = scatter_about(seeds[0], (RECS, FRAMES, D), 1.0, 6.0, ((0, 16), (1, 32)))
    gate_probs = jnp.clip(0.05 + 0.9 * jax.random.uniform(seeds[1], (RECS, TOP, FRAMES), jnp.float32) ** steps_of(seeds[1], (RECS, TOP, FRAMES), ((0, 16), (2, 32)), -0.2, 0.2), 0.05, 0.95)
    expert_ids = draw_expert_ids(jax.random.fold_in(seeds[9], 71), 0)
    slot_ids = draw_slot_ids(jax.random.fold_in(seeds[9], 71), 0)
    mask_pos = draw_mask_pos(jax.random.fold_in(seeds[9], 71), 0)
    distractors = draw_distractors(jax.random.fold_in(seeds[9], 71), 0)
    targets = scatter_about(seeds[6], (RECS, MASKED, D), 1.0, 6.0, ((0, 16), (1, 32)))
    weight_in = scatter_about(seeds[7], (EXPERTS, D, FF), D ** -0.5, 0.15625, ((0, 32), (2, 16)))
    weight_out = scatter_about(seeds[8], (EXPERTS, FF, D), FF ** -0.5, 0.078125, ((0, 32), (1, 16)))
    return dict(hidden=hidden, gate_probs=gate_probs, expert_ids=expert_ids, slot_ids=slot_ids, mask_pos=mask_pos, distractors=distractors, targets=targets, weight_in=weight_in, weight_out=weight_out)


sharpness_divisor = 0.1
objective_scaling = 64.0
norm_eps = 1e-06

def gelu_slope(preact):
    return jax.vjp(jax.nn.gelu, preact)[1](jnp.ones_like(preact))[0]

def slot_tables(expert_picks, slot_picks, gate_values, experts_all):
    kept_mask = slot_picks < CAP
    slot_width = experts_all * CAP
    slot_index = jnp.where(kept_mask, expert_picks * CAP + slot_picks, slot_width)
    matches = slot_index[:, :, None] == jnp.arange(slot_width, dtype=jnp.int32)[None, None, :]
    frame_count = expert_picks.shape[1]
    frame_iota = jnp.arange(frame_count, dtype=jnp.int32)
    slot_frame = lax.optimization_barrier(jnp.sum(jnp.where(matches, frame_iota[None, :, None], 0), axis=(0, 1))).astype(jnp.int32)
    slot_gate = lax.optimization_barrier(jnp.sum(jnp.where(matches, gate_values[:, :, None], 0.0), axis=(0, 1)))
    return (kept_mask, jnp.minimum(slot_index, slot_width - 1).astype(jnp.int32), slot_frame, slot_gate)

def contrast_loss(context, own_targets, fetched):
    context_norm = jnp.sqrt(lax.optimization_barrier(jnp.sum(context * context, axis=-1)) + norm_eps)
    context_unit = context / context_norm[:, None]
    candidates = jnp.concatenate([own_targets[None], fetched], axis=0).astype(jnp.float32)
    target_norm = jnp.sqrt(lax.optimization_barrier(jnp.sum(candidates * candidates, axis=-1)) + norm_eps)
    target_unit = candidates / target_norm[..., None]
    angular_agreement = lax.optimization_barrier(jnp.sum(context_unit[None] * target_unit, axis=-1))
    raw_match_values = angular_agreement / sharpness_divisor
    log_total = jnp.log(lax.optimization_barrier(jnp.sum(jnp.exp(raw_match_values), axis=0)))
    frame_loss = log_total - raw_match_values[0]
    normalized_exponential_share = jnp.exp(raw_match_values - log_total[None])
    correct_match_value = (jnp.arange(raw_match_values.shape[0]) == 0).astype(jnp.float32)[:, None]
    raw_match_derivative_scaling = objective_scaling * (normalized_exponential_share - correct_match_value) / sharpness_divisor
    grad_unit = lax.optimization_barrier(jnp.sum(raw_match_derivative_scaling[..., None] * target_unit, axis=0))
    along = lax.optimization_barrier(jnp.sum(grad_unit * context_unit, axis=-1))
    grad_context = (grad_unit - along[:, None] * context_unit) / context_norm[:, None]
    return (frame_loss, grad_context)

def take_rows(table, where_at):
    return jnp.take(table, where_at, axis=0)

def reference(hidden, gate_probs, expert_ids, slot_ids, mask_pos, distractors, targets, weight_in, weight_out):
    block_size = FF // N_DP
    frame_blocks = hidden.reshape(RECS, N_SEQ, FR_DEV, D)

    def by_block(array):
        return array.reshape(RECS, TOP, N_SEQ, FR_DEV).transpose(0, 2, 1, 3)

    def tables_one(expert_picks, slot_picks, gate_values):
        return slot_tables(expert_picks, slot_picks, gate_values, EXPERTS)
    kept_mask, slot_index, slot_frame, slot_gate = jax.vmap(jax.vmap(tables_one))(by_block(expert_ids), by_block(slot_ids), by_block(gate_probs))
    gate_blocks = by_block(gate_probs)
    place_blocks = mask_pos.reshape(RECS, N_SEQ, M_DEV)
    outgoing = jax.vmap(jax.vmap(take_rows))(frame_blocks, slot_frame)

    def per_expert(array):
        return array.reshape(RECS, N_SEQ, EXPERTS, CAP, D).transpose(2, 0, 1, 3, 4).reshape(EXPERTS, RECS * N_SEQ * CAP, D)

    def per_block(array):
        return array.reshape(EXPERTS, RECS, N_SEQ, CAP, D).transpose(1, 2, 0, 3, 4).reshape(RECS, N_SEQ, EXPERTS * CAP, D)

    def split_sum(partial_value):
        rounded = lax.optimization_barrier(partial_value.astype(jnp.bfloat16))
        return lax.optimization_barrier(jnp.sum(rounded.astype(jnp.float32), axis=0)).astype(jnp.bfloat16)

    def expert_forward(operands):
        row_block, first_weight, second_weight = operands
        preact = jnp.dot(row_block, first_weight, preferred_element_type=jnp.float32)
        activation = jax.nn.gelu(preact).astype(jnp.bfloat16)
        partial_value = jnp.einsum('rnh,nhd->nrd', activation.reshape(-1, N_DP, block_size).astype(jnp.float32), second_weight.reshape(N_DP, block_size, D).astype(jnp.float32))
        return split_sum(partial_value)
    expert_out = per_block(lax.map(expert_forward, (per_expert(outgoing), weight_in, weight_out)))

    def recording_front(operands):
        frame_block, returned, kept_block, slot_block, gate_values, frame_of, gate_of, places, own_targets, wanted = operands
        picked = jax.vmap(take_rows)(returned, slot_block.reshape(N_SEQ, -1))
        picked = picked.reshape(N_SEQ, TOP, FR_DEV, D).astype(jnp.float32)
        weight = jnp.where(kept_block, gate_values, 0.0)
        mixed_rows = (frame_block.astype(jnp.float32) + lax.optimization_barrier(jnp.sum(weight[..., None] * picked, axis=1))).astype(jnp.bfloat16)
        context = jax.vmap(take_rows)(mixed_rows, places).astype(jnp.float32).reshape(MASKED, D)
        fetched = jnp.take(own_targets, wanted.reshape(-1), axis=0).reshape(NEG, MASKED, D)
        frame_loss, grad_context = contrast_loss(context, own_targets, fetched)

        def spread(values, where_at):
            return jnp.zeros((FR_DEV, D), jnp.float32).at[where_at].set(values)
        grad_mixed = jax.vmap(spread)(grad_context.reshape(N_SEQ, M_DEV, D), places)
        gate_grad = jnp.where(kept_block, lax.optimization_barrier(jnp.sum(grad_mixed[:, None] * picked, axis=-1)), 0.0)
        grad_out = (jax.vmap(take_rows)(grad_mixed, frame_of) * gate_of[..., None]).astype(jnp.bfloat16)
        return (frame_loss, gate_grad, grad_out, grad_mixed)
    frame_loss, gate_grad, grad_out, grad_mixed = lax.map(recording_front, (frame_blocks, expert_out, kept_mask, slot_index, gate_blocks, slot_frame, slot_gate, place_blocks, targets, distractors))
    gate_grad = gate_grad.transpose(0, 2, 1, 3).reshape(RECS, TOP, FRAMES)

    def expert_backward(operands):
        row_block, grad_block, first_weight, second_weight = operands
        preact = jnp.dot(row_block, first_weight, preferred_element_type=jnp.float32)
        activation = jax.nn.gelu(preact).astype(jnp.bfloat16)
        grad_act = jnp.dot(grad_block, second_weight.T, preferred_element_type=jnp.float32)
        grad_pre = (grad_act * gelu_slope(preact)).astype(jnp.bfloat16)
        grad_second = jnp.dot(activation.T, grad_block, preferred_element_type=jnp.float32).astype(jnp.bfloat16)
        grad_first = jnp.dot(row_block.T, grad_pre, preferred_element_type=jnp.float32).astype(jnp.bfloat16)
        partial_value = jnp.einsum('rnh,dnh->nrd', grad_pre.reshape(-1, N_DP, block_size).astype(jnp.float32), first_weight.reshape(D, N_DP, block_size).astype(jnp.float32))
        return (grad_first, grad_second, split_sum(partial_value))
    grad_weight_in, grad_weight_out, grad_rows = lax.map(expert_backward, (per_expert(outgoing), per_expert(grad_out), weight_in, weight_out))
    grad_back = per_block(grad_rows)

    def recording_back(operands):
        grad_block, back_rows, kept_block, slot_block = operands
        grad_inputs = jax.vmap(take_rows)(back_rows, slot_block.reshape(N_SEQ, -1))
        grad_inputs = grad_inputs.reshape(N_SEQ, TOP, FR_DEV, D).astype(jnp.float32)
        added = lax.optimization_barrier(jnp.sum(jnp.where(kept_block[..., None], grad_inputs, 0.0), axis=1))
        return (grad_block + added).astype(jnp.bfloat16)
    grad_hidden = lax.map(recording_back, (grad_mixed, grad_back, kept_mask, slot_index)).reshape(RECS, FRAMES, D)
    return (frame_loss, gate_grad, grad_hidden, grad_weight_in, grad_weight_out)
```

```python
import jax
import jax.numpy as jnp
from jax import lax
from jax.experimental import pallas as pl
from jax.experimental.pallas import tpu as pltpu
from jax.sharding import PartitionSpec as P

MESH = pl.DeviceIdType.MESH
BF = jnp.bfloat16
F32 = jnp.float32
NZ = 16
NS = 32
CHUNKS = 4
D = 1280
HID = 320
ROWS = 64
FR = 128
MK = 64
NEG = 10
EPS = 1e-06
SHARP = 0.1
SCALE = 64.0
DZ = [0] + [(h + 1) // 2 if h % 2 else NZ - h // 2 for h in range(1, NZ)]


def dot(a, b):
    return jnp.dot(a, b, preferred_element_type=F32)


def dot_nt(a, b):
    return lax.dot_general(a, b, (((1,), (1,)), ((), ())), preferred_element_type=F32)


def pieces(v):
    hi = v.astype(BF)
    lo = (v - hi.astype(F32)).astype(BF)
    return hi, lo


def gelu_parts(x):
    k = 0.7978845608028654
    x2 = x * x
    t = jnp.tanh(k * (x + 0.044715 * (x2 * x)))
    half = 0.5 * (1.0 + t)
    slope = half + 0.5 * x * (1.0 - t * t) * (k * (1.0 + (3 * 0.044715) * x2))
    return x * half, slope


def kernel(
    hid_ref, gate_ref, exp_ref, slot_ref, pos_ref, dis_ref, tgt_ref, win_ref, wout_ref,
    loss_ref, gg_ref, gh_ref, dwi_ref, dwo_ref,
    hid, gate, exps, slots, pos, dis, win, wout, wint, woutt,
    tgt, out, inn, grp, part, rsb, acc, rsa, rout, ret,
    act_t, grp_t, slope, gpre, lossv, ggv, ghv, dwiv, dwov,
    lsem, osem,
    ds, dr, gas, gar, gbs, gbr, bs, br, as_, ar, ts, tr,
    rgs, rgr, sbs, sbr,
):
    dp, s = lax.axis_index("dp"), lax.axis_index("seq")
    z, c = s // 2, s % 2
    y, x = dp // 4, dp % 4
    a = x + c * (y - x)
    b = y + c * (x - y)

    def dpi(aa, bb):
        return aa * (1 + 3 * c) + bb * (4 - 3 * c)

    apeer = {d: (dpi((a + d) % 4, b), s) for d in (1, 2, 3)}
    bpeer = {d: (dpi(a, (b + d) % 4), s) for d in (1, 2, 3)}

    def zpeer(k):
        return (dp, ((z + NZ - DZ[k // 2]) % NZ) * 2 + (c + k % 2) % 2)

    def zback(k):
        return (dp, ((z + DZ[k // 2]) % NZ) * 2 + (c + k % 2) % 2)

    zup = (dp, ((z + 1) % NZ) * 2 + c)
    zdn = (dp, ((z + NZ - 1) % NZ) * 2 + c)
    sib = (dp, z * 2 + 1 - c)

    def rc(src, dst, ssem, rsem, dev):
        return pltpu.make_async_remote_copy(
            src_ref=src, dst_ref=dst, send_sem=ssem, recv_sem=rsem, device_id=dev, device_id_type=MESH
        )

    barrier = pltpu.get_barrier_semaphore()
    for k in range(1, NS):
        pl.semaphore_signal(barrier, inc=1, device_id=zpeer(k), device_id_type=MESH)
    for d in (1, 2, 3):
        pl.semaphore_signal(barrier, inc=1, device_id=apeer[d], device_id_type=MESH)
        pl.semaphore_signal(barrier, inc=1, device_id=bpeer[d], device_id_type=MESH)

    loads = [
        (hid_ref, hid), (gate_ref, gate), (exp_ref, exps), (slot_ref, slots), (pos_ref, pos),
        (dis_ref, dis), (win_ref, win), (wout_ref, wout),
    ]
    loads = [pltpu.make_async_copy(p, q, lsem.at[i]) for i, (p, q) in enumerate(loads)]
    tloads = [
        pltpu.make_async_copy(tgt_ref.at[pl.ds(32 * h, 32)], tgt.at[z, c, h], lsem.at[len(loads) + h])
        for h in (0, 1)
    ]
    for cp in loads + tloads:
        cp.start()
    for cp in loads[:5]:
        cp.wait()

    row = lax.broadcasted_iota(jnp.int32, (ROWS, FR), 0)
    kk = row >> 1
    hh = kk >> 1
    dz = jnp.where((hh & 1) == 1, (hh + 1) >> 1, (NZ - (hh >> 1)) & (NZ - 1))
    want = (((z + NZ - dz) & (NZ - 1)) << 1) + ((c + (kk & 1)) & 1)
    cap = row & 1
    own_row = [
        jnp.where((exps[t : t + 1, :] == want) & (slots[t : t + 1, :] == cap), 1.0, 0.0) for t in (0, 1)
    ]
    gate_row = jnp.sum(
        own_row[0] * gate[0:1, :] + own_row[1] * gate[1:2, :], axis=1, keepdims=True
    )
    disp = own_row[0] + own_row[1]
    disp_b = disp.astype(BF)
    disp_t = disp.T.astype(BF)
    spread = jnp.where(lax.broadcasted_iota(jnp.int32, (FR, MK), 0) == pos[0:1, :], 1.0, 0.0)
    spread_b = spread.astype(BF)
    pick_b = spread.T.astype(BF)
    mrow_t = dot(disp_b, spread_b)

    def put_out(p, rows):
        for k in range(NS):
            out[p, k] = rows[2 * k : 2 * k + 2].astype(BF)

    def send_out(p):
        for k in range(1, NS):
            rc(out.at[p, k], inn.at[p, k], ds.at[p, k // 8], dr.at[p, k // 8], zpeer(k)).start()
        inn[p, 0] = out[p, 0]

    def span(ch):
        return pl.ds(8 * ch, 8) if ch else pl.ds(1, 7)

    def gather_in(p, ch):
        rc(out.at[p, span(ch)], inn.at[p, span(ch)], ds.at[p, ch], dr.at[p, ch], zup).wait_recv()
        rows = inn[p, 8 * ch : 8 * ch + 8].astype(F32).reshape(16, D).astype(BF)
        grp[p, ch, b, a] = rows
        blk = grp.at[p, ch, b, a]
        for d in (1, 2, 3):
            rc(blk, blk, gas.at[p, ch, d - 1], gar.at[p, ch, d - 1], apeer[d]).start()

    def gather_mid(p, ch):
        for d in (1, 2, 3):
            blk = grp.at[p, ch, b, (a + 4 - d) % 4]
            rc(blk, blk, gas.at[p, ch, d - 1], gar.at[p, ch, d - 1], apeer[d]).wait_recv()
        blk = grp.at[p, ch, b]
        for d in (1, 2, 3):
            rc(blk, blk, gbs.at[p, ch, d - 1], gbr.at[p, ch, d - 1], bpeer[d]).start()

    def work(p, ch):
        for d in (1, 2, 3):
            blk = grp.at[p, ch, (b + 4 - d) % 4]
            rc(blk, blk, gbs.at[p, ch, d - 1], gbr.at[p, ch, d - 1], bpeer[d]).wait_recv()
        rows = grp[p, ch].reshape(256, D)
        if p == 0:
            act, slp = gelu_parts(dot(rows, win[...]))
            act = act.astype(BF)
            part[p, ch] = dot(act, wout[...]).astype(BF).reshape(4, 4, 16, D)
        else:
            grad_pre = (dot(rows, woutt[...]) * slope[pl.ds(256 * ch, 256), :]).astype(BF)
            part[p, ch] = dot(grad_pre, wint[...]).astype(BF).reshape(4, 4, 16, D)
        for d in (1, 2, 3):
            rc(
                part.at[p, ch, (b + d) % 4], rsb.at[p, ch, d - 1], bs.at[p, ch, d - 1], br.at[p, ch, d - 1],
                bpeer[d],
            ).start()
        if p == 0:
            slope[pl.ds(256 * ch, 256), :] = slp
            act_t[:, 256 * ch : 256 * ch + 256] = act.T
            grp_t[:, 256 * ch : 256 * ch + 256] = rows.T
        else:
            gpre[pl.ds(256 * ch, 256), :] = grad_pre

    def reduce_b(p, ch):
        for d in (1, 2, 3):
            rc(
                part.at[p, ch, (b + d) % 4], rsb.at[p, ch, d - 1], bs.at[p, ch, d - 1], br.at[p, ch, d - 1],
                bpeer[d],
            ).wait_recv()
        total = (part[p, ch, b].astype(F32) + rsb[p, ch, 0].astype(F32)) + (
            rsb[p, ch, 1].astype(F32) + rsb[p, ch, 2].astype(F32)
        )
        acc[p, ch] = total.astype(BF)
        for d in (1, 2, 3):
            rc(
                acc.at[p, ch, (a + d) % 4], rsa.at[p, ch, d - 1], as_.at[p, ch, d - 1], ar.at[p, ch, d - 1],
                apeer[d],
            ).start()

    def reduce_a(p, ch):
        for d in (1, 2, 3):
            rc(
                acc.at[p, ch, (a + d) % 4], rsa.at[p, ch, d - 1], as_.at[p, ch, d - 1], ar.at[p, ch, d - 1],
                apeer[d],
            ).wait_recv()
        total = (acc[p, ch, a].astype(F32) + rsa[p, ch, 0].astype(F32)) + (
            rsa[p, ch, 1].astype(F32) + rsa[p, ch, 2].astype(F32)
        )
        rout[p, 8 * ch : 8 * ch + 8] = total.reshape(8, 2, D).astype(BF)
        for k in range(8 * ch, 8 * ch + 8):
            if k:
                rc(rout.at[p, k], ret.at[p, k], ts.at[p, ch], tr.at[p, ch], zback(k)).start()
        if ch == 0:
            ret[p, 0] = rout[p, 0]

    def returned(p):
        for ch in range(CHUNKS):
            rc(rout.at[p, span(ch)], ret.at[p, span(ch)], ts.at[p, ch], tr.at[p, ch], zup).wait_recv()
        return ret[p].astype(F32).reshape(ROWS, D).astype(BF)

    def sends_done(p):
        for ch in range(CHUNKS):
            rc(out.at[p, span(ch)], inn.at[p, span(ch)], ds.at[p, ch], dr.at[p, ch], zup).wait_send()
            rc(rout.at[p, span(ch)], ret.at[p, span(ch)], ts.at[p, ch], tr.at[p, ch], zup).wait_send()
            for d in (1, 2, 3):
                blk = grp.at[p, ch, b, a]
                rc(blk, blk, gas.at[p, ch, d - 1], gar.at[p, ch, d - 1], apeer[d]).wait_send()
                blk = grp.at[p, ch, b]
                rc(blk, blk, gbs.at[p, ch, d - 1], gbr.at[p, ch, d - 1], bpeer[d]).wait_send()
                rc(
                    part.at[p, ch, (b + d) % 4], rsb.at[p, ch, d - 1], bs.at[p, ch, d - 1],
                    br.at[p, ch, d - 1], bpeer[d],
                ).wait_send()
                rc(
                    acc.at[p, ch, (a + d) % 4], rsa.at[p, ch, d - 1], as_.at[p, ch, d - 1],
                    ar.at[p, ch, d - 1], apeer[d],
                ).wait_send()

    def ring_at(u):
        step, half = u // 2, u % 2
        up_half = half if u < 14 else 0
        dn_half = half if u < 14 else 1
        return step, up_half, dn_half

    def ring_copy(u, way):
        step, up_half, dn_half = ring_at(u)
        if way == 0:
            blk = tgt.at[(z + NZ - step) % NZ, c, up_half]
            return rc(blk, blk, rgs.at[0, u], rgr.at[0, u], zup)
        blk = tgt.at[(z + step) % NZ, c, dn_half]
        return rc(blk, blk, rgs.at[1, u], rgr.at[1, u], zdn)

    def ring_got(u, way):
        step, up_half, dn_half = ring_at(u)
        if way == 0:
            return tgt.at[(z + NZ - 1 - step) % NZ, c, up_half]
        return tgt.at[(z + 1 + step) % NZ, c, dn_half]

    def ring_take(u):
        for way in (0, 1):
            blk = ring_got(u, way)
            rc(blk, blk, rgs.at[way, u], rgr.at[way, u], zup).wait_recv()
            n = 2 + 2 * u + way
            rc(blk, blk, sbs.at[n], sbr.at[n], sib).start()

    def ring_step(u):
        if u == 0:
            for h in (0, 1):
                tloads[h].wait()
                blk = tgt.at[z, c, h]
                rc(blk, blk, sbs.at[h], sbr.at[h], sib).start()
        if 2 <= u != 15:
            ring_take(u - 2)
        if u == 14:
            ring_take(13)
        if u < 15:
            ring_copy(u, 0).start()
            ring_copy(u, 1).start()

    ring_next = [0]

    def ring_some(n):
        for _ in range(n):
            if ring_next[0] < 17:
                ring_step(ring_next[0])
                ring_next[0] += 1

    def shared_done():
        for h in (0, 1):
            blk = tgt.at[z, 1 - c, h]
            rc(blk, blk, sbs.at[h], sbr.at[h], sib).wait_recv()
        for u in range(15):
            step, up_half, dn_half = ring_at(u)
            for way in (0, 1):
                pos_z = (z + NZ - 1 - step) % NZ if way == 0 else (z + 1 + step) % NZ
                blk = tgt.at[pos_z, 1 - c, up_half if way == 0 else dn_half]
                n = 2 + 2 * u + way
                rc(blk, blk, sbs.at[n], sbr.at[n], sib).wait_recv()

    def ring_sends_done():
        for u in range(15):
            for way in (0, 1):
                ring_copy(u, way).wait_send()
                blk = ring_got(u, way)
                n = 2 + 2 * u + way
                rc(blk, blk, sbs.at[n], sbr.at[n], sib).wait_send()
        for h in (0, 1):
            blk = tgt.at[z, c, h]
            rc(blk, blk, sbs.at[h], sbr.at[h], sib).wait_send()

    stages = (gather_in, gather_mid, work, reduce_b, reduce_a)

    def flow(p):
        for t in range(CHUNKS + len(stages) - 1):
            for i in reversed(range(len(stages))):
                if 0 <= t - i < CHUNKS:
                    stages[i](p, t - i)
                    if p == 0 and t >= 1:
                        ring_some(1)

    put_out(0, dot(disp_b, hid[...]))
    pl.semaphore_wait(barrier, NS - 1 + 6)
    send_out(0)
    for cp in loads[5:]:
        cp.wait()
    picked_hidden = dot(pick_b, hid[...])
    wint[...] = win[...].T
    woutt[...] = wout[...].T
    flow(0)
    ring_some(17)

    lane = lax.broadcasted_iota(jnp.int32, (MK, NS * MK), 1)
    sub = lax.broadcasted_iota(jnp.int32, (MK, NS * MK), 0)
    own = jnp.where(lane == sub + s * MK, 1.0, 0.0)
    dis_f = jnp.concatenate([dis[...].astype(F32), jnp.zeros((16 - NEG, MK), F32)], axis=0).T
    lane_f = lane.astype(F32)
    count = own
    for j in range(NEG):
        count = count + jnp.where(dis_f[:, j : j + 1] == lane_f, 1.0, 0.0)
    shared_done()
    norms = []
    for q in range(NZ):
        v = tgt[q].reshape(2 * MK, D).astype(F32)
        n2 = jnp.sum(v * v, axis=1, keepdims=True)
        norms.append(jnp.broadcast_to(n2, (2 * MK, 128)).T[0:1, :])
    t_inv = 1.0 / jnp.sqrt(jnp.concatenate(norms, axis=1) + EPS)

    eout = returned(0)
    coef = (mrow_t * gate_row).T
    c_hi, c_lo = pieces(coef)
    mixed = picked_hidden + (dot(c_hi, eout) + dot(c_lo, eout))
    ctx_b = mixed.astype(BF)
    ctx = ctx_b.astype(F32)
    c_inv = 1.0 / jnp.sqrt(jnp.sum(ctx * ctx, axis=1, keepdims=True) + EPS)
    everyone = tgt[...].reshape(NS * MK, D)
    logits = dot_nt(ctx_b, everyone) * (c_inv * (1.0 / SHARP)) * t_inv
    log_total = jnp.log(jnp.sum(count * jnp.exp(logits), axis=1, keepdims=True))
    loss = log_total - jnp.sum(own * logits, axis=1, keepdims=True)
    lossv[:, :MK] = jnp.broadcast_to(loss, (MK, 128)).T[0:1, :]
    share = count * jnp.exp(logits - log_total)
    coef = (share - own) * (SCALE / SHARP) * t_inv
    c_hi, c_lo = pieces(coef)
    grad_unit = dot(c_hi, everyone) + dot(c_lo, everyone)
    ctx_unit = ctx * c_inv
    along = jnp.sum(grad_unit * ctx_unit, axis=1, keepdims=True)
    grad_ctx = (grad_unit - along * ctx_unit) * c_inv
    g_hi, g_lo = pieces(grad_ctx)
    g_two = jnp.concatenate([g_hi, g_lo], axis=0)

    mrow_b = mrow_t.astype(BF)
    grad_rows = dot(jnp.concatenate([mrow_b, mrow_b], axis=1), g_two) * gate_row
    put_out(1, grad_rows)
    send_out(1)
    q_two = dot_nt(eout, g_two)
    q_row = jnp.sum(mrow_t * (q_two[:, :MK] + q_two[:, MK:]), axis=1, keepdims=True)
    for t in (0, 1):
        ggv[t : t + 1, :] = jnp.sum(own_row[t] * q_row, axis=0, keepdims=True)
    grad_mixed = dot(jnp.concatenate([spread_b, spread_b], axis=1), g_two)
    outs = [
        pltpu.make_async_copy(lossv.at[:, pl.ds(0, 128)], loss_ref, osem.at[0]),
        pltpu.make_async_copy(ggv, gg_ref, osem.at[1]),
        pltpu.make_async_copy(dwov, dwo_ref, osem.at[2]),
        pltpu.make_async_copy(dwiv, dwi_ref, osem.at[3]),
        pltpu.make_async_copy(ghv, gh_ref, osem.at[4]),
    ]
    outs[0].start()
    outs[1].start()
    flow(1)

    grads = grp[1].reshape(16 * ROWS, D)
    for n in range(5):
        dwov[:, 256 * n : 256 * n + 256] = dot(act_t[...], grads[:, 256 * n : 256 * n + 256]).astype(BF)
    outs[2].start()
    gp = gpre[...]
    for n in range(5):
        dwiv[256 * n : 256 * n + 256, :] = dot(grp_t[256 * n : 256 * n + 256, :], gp).astype(BF)
    outs[3].start()
    ghv[...] = (grad_mixed + dot(disp_t, returned(1))).astype(BF)
    outs[4].start()
    ring_sends_done()
    sends_done(0)
    sends_done(1)
    for cp in outs:
        cp.wait()


def local(
    hidden, gate_probs, expert_ids, slot_ids, mask_pos, distractors, targets, weight_in, weight_out
):
    dma = pltpu.SemaphoreType.DMA
    vm = pltpu.VMEM
    hbm = pl.BlockSpec(memory_space=pl.ANY)
    outs = pl.pallas_call(
        kernel,
        out_shape=(
            jax.ShapeDtypeStruct((1, 128), F32),
            jax.ShapeDtypeStruct((2, FR), F32),
            jax.ShapeDtypeStruct((FR, D), BF),
            jax.ShapeDtypeStruct((D, HID), BF),
            jax.ShapeDtypeStruct((HID, D), BF),
        ),
        in_specs=[hbm] * 9,
        out_specs=(hbm,) * 5,
        scratch_shapes=[
            vm((FR, D), BF),
            vm((2, FR), F32),
            vm((2, FR), jnp.int32),
            vm((2, FR), jnp.int32),
            vm((1, MK), jnp.int32),
            vm((NEG, MK), jnp.int32),
            vm((D, HID), BF),
            vm((HID, D), BF),
            vm((HID, D), BF),
            vm((D, HID), BF),
            vm((NZ, 2, 2, 32, D), BF),
            vm((2, NS, 2, D), BF),
            vm((2, NS, 2, D), BF),
            vm((2, CHUNKS, 4, 4, 16, D), BF),
            vm((2, CHUNKS, 4, 4, 16, D), BF),
            vm((2, CHUNKS, 3, 4, 16, D), BF),
            vm((2, CHUNKS, 4, 16, D), BF),
            vm((2, CHUNKS, 3, 16, D), BF),
            vm((2, NS, 2, D), BF),
            vm((2, NS, 2, D), BF),
            vm((HID, 16 * ROWS), BF),
            vm((D, 16 * ROWS), BF),
            vm((16 * ROWS, HID), F32),
            vm((16 * ROWS, HID), BF),
            vm((1, 128), F32),
            vm((2, FR), F32),
            vm((FR, D), BF),
            vm((D, HID), BF),
            vm((HID, D), BF),
            dma((10,)),
            dma((5,)),
            dma((2, CHUNKS)),
            dma((2, CHUNKS)),
            dma((2, CHUNKS, 3)),
            dma((2, CHUNKS, 3)),
            dma((2, CHUNKS, 3)),
            dma((2, CHUNKS, 3)),
            dma((2, CHUNKS, 3)),
            dma((2, CHUNKS, 3)),
            dma((2, CHUNKS, 3)),
            dma((2, CHUNKS, 3)),
            dma((2, CHUNKS)),
            dma((2, CHUNKS)),
            dma((2, 15)),
            dma((2, 15)),
            dma((32,)),
            dma((32,)),
        ],
        compiler_params=pltpu.CompilerParams(
            collective_id=0, has_side_effects=True, vmem_limit_bytes=56 * 2**20
        ),
        cost_estimate=pl.CostEstimate(
            flops=6_000_000_000, bytes_accessed=8_000_000, transcendentals=1_000_000
        ),
        name="experts",
    )(
        hidden[0], gate_probs[0], expert_ids[0], slot_ids[0], mask_pos, distractors[0], targets[0],
        weight_in[0], weight_out[0],
    )
    loss, gate_grad, grad_hidden, grad_in, grad_out = outs
    return (loss[:, :MK], gate_grad[None], grad_hidden[None], grad_in[None], grad_out[None])


def solution(mesh):
    return jax.shard_map(
        local,
        mesh=mesh,
        in_specs=(
            P("dp", "seq", None),
            P("dp", None, "seq"),
            P("dp", None, "seq"),
            P("dp", None, "seq"),
            P("dp", "seq"),
            P("dp", None, "seq"),
            P("dp", "seq", None),
            P("seq", None, "dp"),
            P("seq", "dp", None),
        ),
        out_specs=(
            P("dp", "seq"),
            P("dp", None, "seq"),
            P("dp", "seq", None),
            P("seq", None, "dp"),
            P("seq", "dp", None),
        ),
        check_vma=False,
    )
```

```python
import jax
import jax.numpy as jnp
from jax import lax
from jax.experimental import pallas as pl
from jax.experimental.pallas import tpu as pltpu
from jax.sharding import PartitionSpec as P

MESH = pl.DeviceIdType.MESH
BF = jnp.bfloat16
F32 = jnp.float32
NZ = 16
NS = 32
CHUNKS = 4
D = 1280
HID = 320
ROWS = 64
FR = 128
MK = 64
NEG = 10
EPS = 1e-06
SHARP = 0.1
SCALE = 64.0
ORDER = [
    (0, 0), (0, 1), (1, 0), (0, 2), (1, 1), (2, 0), (0, 3), (1, 2), (2, 1), (1, 3), (2, 2), (3, 0),
    (2, 3), (3, 1), (3, 2), (3, 3), (4, 0), (4, 1), (4, 2), (4, 3), (5, 0), (5, 1), (5, 2), (5, 3),
    (6, 0), (6, 1), (6, 2), (6, 3),
]
DZ = [0] + [(h + 1) // 2 if h % 2 else NZ - h // 2 for h in range(1, NZ)]


def dot(a, b):
    return jnp.dot(a, b, preferred_element_type=F32)


def dot_nt(a, b):
    return lax.dot_general(a, b, (((1,), (1,)), ((), ())), preferred_element_type=F32)


def pieces(v):
    hi = v.astype(BF)
    lo = (v - hi.astype(F32)).astype(BF)
    return hi, lo


def gelu_parts(x):
    k = 0.7978845608028654
    x2 = x * x
    t = jnp.tanh(k * (x + 0.044715 * (x2 * x)))
    half = 0.5 * (1.0 + t)
    slope = half + 0.5 * x * (1.0 - t * t) * (k * (1.0 + (3 * 0.044715) * x2))
    return x * half, slope


def kernel(
    hid_ref, gate_ref, exp_ref, slot_ref, pos_ref, dis_ref, tgt_ref, win_ref, wout_ref,
    loss_ref, gg_ref, gh_ref, dwi_ref, dwo_ref,
    hid, gate, exps, slots, pos, dis, win, wout, wint, woutt,
    tgt, out, inn, grp, part, rsb, acc, rsa, rout, ret,
    act_t, slope, gpre_t, lossv, ggv, ghv, dwiv, dwov,
    lsem, osem,
    ds, dr, gas, gar, gbs, gbr, bs, br, as_, ar, ts, tr,
    rgs, rgr, sbs, sbr,
):
    dp, s = lax.axis_index("dp"), lax.axis_index("seq")
    z, c = s // 2, s % 2
    y, x = dp // 4, dp % 4
    a = x + c * (y - x)
    b = y + c * (x - y)

    def dpi(aa, bb):
        return aa * (1 + 3 * c) + bb * (4 - 3 * c)

    apeer = {d: (dpi((a + d) % 4, b), s) for d in (1, 2, 3)}
    bpeer = {d: (dpi(a, (b + d) % 4), s) for d in (1, 2, 3)}

    def zpeer(k):
        return (dp, ((z + NZ - DZ[k // 2]) % NZ) * 2 + (c + k % 2) % 2)

    def zback(k):
        return (dp, ((z + DZ[k // 2]) % NZ) * 2 + (c + k % 2) % 2)

    zup = (dp, ((z + 1) % NZ) * 2 + c)
    zdn = (dp, ((z + NZ - 1) % NZ) * 2 + c)
    sib = (dp, z * 2 + 1 - c)

    def rc(src, dst, ssem, rsem, dev):
        return pltpu.make_async_remote_copy(
            src_ref=src, dst_ref=dst, send_sem=ssem, recv_sem=rsem, device_id=dev, device_id_type=MESH
        )

    loads = [
        (hid_ref, hid), (gate_ref, gate), (exp_ref, exps), (slot_ref, slots), (pos_ref, pos),
        (dis_ref, dis), (win_ref, wint), (wout_ref, wout),
    ]
    loads = [pltpu.make_async_copy(p, q, lsem.at[i]) for i, (p, q) in enumerate(loads)]
    tloads = [
        pltpu.make_async_copy(tgt_ref.at[pl.ds(32 * h, 32)], tgt.at[z, c, h], lsem.at[len(loads) + h])
        for h in (0, 1)
    ]
    for cp in loads + tloads:
        cp.start()
    barrier = pltpu.get_barrier_semaphore()
    for k in range(1, NS):
        pl.semaphore_signal(barrier, inc=1, device_id=zpeer(k), device_id_type=MESH)
    for d in (1, 2, 3):
        pl.semaphore_signal(barrier, inc=1, device_id=apeer[d], device_id_type=MESH)
        pl.semaphore_signal(barrier, inc=1, device_id=bpeer[d], device_id_type=MESH)

    for cp in loads[:5]:
        cp.wait()

    row = lax.broadcasted_iota(jnp.int32, (ROWS, FR), 0)
    kk = row >> 1
    hh = kk >> 1
    dz = jnp.where((hh & 1) == 1, (hh + 1) >> 1, (NZ - (hh >> 1)) & (NZ - 1))
    want = (((z + NZ - dz) & (NZ - 1)) << 1) + ((c + (kk & 1)) & 1)
    cap = row & 1
    own_row = [
        jnp.where((exps[t : t + 1, :] == want) & (slots[t : t + 1, :] == cap), 1.0, 0.0) for t in (0, 1)
    ]
    gate_row = jnp.sum(
        own_row[0] * gate[0:1, :] + own_row[1] * gate[1:2, :], axis=1, keepdims=True
    )
    disp = own_row[0] + own_row[1]
    disp_b = disp.astype(BF)
    disp_t = disp.T.astype(BF)
    spread = jnp.where(lax.broadcasted_iota(jnp.int32, (FR, MK), 0) == pos[0:1, :], 1.0, 0.0)
    spread_b = spread.astype(BF)
    pick_b = spread.T.astype(BF)
    mrow_t = dot(disp_b, spread_b)

    def put_out(p, rows):
        for k in range(NS):
            out[p, k] = rows[2 * k : 2 * k + 2].astype(BF)

    def send_out(p):
        for k in range(1, NS):
            rc(out.at[p, k], inn.at[p, k], ds.at[p, k // 8], dr.at[p, k // 8], zpeer(k)).start()
        inn[p, 0] = out[p, 0]

    def span(ch):
        return pl.ds(8 * ch, 8) if ch else pl.ds(1, 7)

    def gather_in(p, ch):
        rc(out.at[p, span(ch)], inn.at[p, span(ch)], ds.at[p, ch], dr.at[p, ch], zup).wait_recv()
        rows = inn[p, 8 * ch : 8 * ch + 8].astype(F32).reshape(16, D).astype(BF)
        grp[p, ch, b, a] = rows
        blk = grp.at[p, ch, b, a]
        for d in (1, 2, 3):
            rc(blk, blk, gas.at[p, ch, d - 1], gar.at[p, ch, d - 1], apeer[d]).start()

    def gather_mid(p, ch):
        for d in (1, 2, 3):
            blk = grp.at[p, ch, b, (a + 4 - d) % 4]
            rc(blk, blk, gas.at[p, ch, d - 1], gar.at[p, ch, d - 1], apeer[d]).wait_recv()
        for slot in (0, 1):
            b_copy(p, ch, slot).start()

    def fore(ch):
        return 1 if ch % 2 == 0 else 3

    def b_copy(p, ch, slot):
        g = fore(ch)
        blk = grp.at[p, ch, (b + 4 - g) % 4] if slot == 2 else grp.at[p, ch, b]
        dev = bpeer[4 - g] if slot == 1 else bpeer[g]
        return rc(blk, blk, gbs.at[p, ch, slot], gbr.at[p, ch, slot], dev)

    def b_wait(p, ch, slot):
        g = fore(ch)
        blk = grp.at[p, ch, (b + (4 - g, g, 2)[slot]) % 4]
        rc(blk, blk, gbs.at[p, ch, slot], gbr.at[p, ch, slot], bpeer[g]).wait_recv()

    def gather_on(p, ch):
        b_wait(p, ch, 0)
        b_copy(p, ch, 2).start()

    def sum_copy(p, ch, slot):
        g = fore(ch)
        blk = part.at[p, ch, (b + (2, 4 - g, g)[slot]) % 4]
        dev = bpeer[4 - g] if slot == 1 else bpeer[g]
        return rc(blk, rsb.at[p, ch, slot], bs.at[p, ch, slot], br.at[p, ch, slot], dev)

    def work(p, ch):
        b_wait(p, ch, 1)
        b_wait(p, ch, 2)
        rows = grp[p, ch].reshape(256, D)
        if p == 0:
            act, slp = gelu_parts(dot(rows, win[...]))
            act = act.astype(BF)
            part[p, ch] = dot(act, wout[...]).astype(BF).reshape(4, 4, 16, D)
        else:
            grad_pre = (dot(rows, woutt[...]) * slope[pl.ds(256 * ch, 256), :]).astype(BF)
            part[p, ch] = dot(grad_pre, wint[...]).astype(BF).reshape(4, 4, 16, D)
        sum_copy(p, ch, 0).start()
        sum_copy(p, ch, 1).start()
        if p == 0:
            slope[pl.ds(256 * ch, 256), :] = slp
            act_t[:, 256 * ch : 256 * ch + 256] = act.T
        else:
            gpre_t[:, 256 * ch : 256 * ch + 256] = grad_pre.T

    def reduce_on(p, ch):
        nxt = (b + fore(ch)) % 4
        sum_copy(p, ch, 0).wait_recv()
        part[p, ch, nxt] = (part[p, ch, nxt].astype(F32) + rsb[p, ch, 0].astype(F32)).astype(BF)
        sum_copy(p, ch, 2).start()

    def reduce_b(p, ch):
        sum_copy(p, ch, 1).wait_recv()
        sum_copy(p, ch, 2).wait_recv()
        total = part[p, ch, b].astype(F32) + (rsb[p, ch, 1].astype(F32) + rsb[p, ch, 2].astype(F32))
        acc[p, ch] = total.astype(BF)
        for d in (1, 2, 3):
            rc(
                acc.at[p, ch, (a + d) % 4], rsa.at[p, ch, d - 1], as_.at[p, ch, d - 1], ar.at[p, ch, d - 1],
                apeer[d],
            ).start()

    def reduce_a(p, ch):
        for d in (1, 2, 3):
            rc(
                acc.at[p, ch, (a + d) % 4], rsa.at[p, ch, d - 1], as_.at[p, ch, d - 1], ar.at[p, ch, d - 1],
                apeer[d],
            ).wait_recv()
        total = (acc[p, ch, a].astype(F32) + rsa[p, ch, 0].astype(F32)) + (
            rsa[p, ch, 1].astype(F32) + rsa[p, ch, 2].astype(F32)
        )
        rout[p, 8 * ch : 8 * ch + 8] = total.reshape(8, 2, D).astype(BF)
        for k in range(8 * ch, 8 * ch + 8):
            if k:
                rc(rout.at[p, k], ret.at[p, k], ts.at[p, ch], tr.at[p, ch], zback(k)).start()
        if ch == 0:
            ret[p, 0] = rout[p, 0]

    def returned(p):
        for ch in range(CHUNKS):
            rc(rout.at[p, span(ch)], ret.at[p, span(ch)], ts.at[p, ch], tr.at[p, ch], zup).wait_recv()
        return ret[p].astype(F32).reshape(ROWS, D).astype(BF)

    def sends_done(p):
        for ch in range(CHUNKS):
            rc(out.at[p, span(ch)], inn.at[p, span(ch)], ds.at[p, ch], dr.at[p, ch], zup).wait_send()
            rc(rout.at[p, span(ch)], ret.at[p, span(ch)], ts.at[p, ch], tr.at[p, ch], zup).wait_send()
            for d in (1, 2, 3):
                blk = grp.at[p, ch, b, a]
                rc(blk, blk, gas.at[p, ch, d - 1], gar.at[p, ch, d - 1], apeer[d]).wait_send()
                b_copy(p, ch, d - 1).wait_send()
                sum_copy(p, ch, d - 1).wait_send()
                rc(
                    acc.at[p, ch, (a + d) % 4], rsa.at[p, ch, d - 1], as_.at[p, ch, d - 1],
                    ar.at[p, ch, d - 1], apeer[d],
                ).wait_send()

    def ring_at(u):
        step, half = u // 2, u % 2
        up_half = half if u < 14 else 0
        dn_half = half if u < 14 else 1
        return step, up_half, dn_half

    def ring_copy(u, way):
        step, up_half, dn_half = ring_at(u)
        if way == 0:
            blk = tgt.at[(z + NZ - step) % NZ, c, up_half]
            return rc(blk, blk, rgs.at[0, u], rgr.at[0, u], zup)
        blk = tgt.at[(z + step) % NZ, c, dn_half]
        return rc(blk, blk, rgs.at[1, u], rgr.at[1, u], zdn)

    def ring_got(u, way):
        step, up_half, dn_half = ring_at(u)
        if way == 0:
            return tgt.at[(z + NZ - 1 - step) % NZ, c, up_half]
        return tgt.at[(z + 1 + step) % NZ, c, dn_half]

    def ring_take(u):
        for way in (0, 1):
            blk = ring_got(u, way)
            rc(blk, blk, rgs.at[way, u], rgr.at[way, u], zup).wait_recv()
            n = 2 + 2 * u + way
            rc(blk, blk, sbs.at[n], sbr.at[n], sib).start()

    def ring_step(u):
        if u == 0:
            for h in (0, 1):
                tloads[h].wait()
                blk = tgt.at[z, c, h]
                rc(blk, blk, sbs.at[h], sbr.at[h], sib).start()
        if 2 <= u != 15:
            ring_take(u - 2)
        if u == 14:
            ring_take(13)
        if u < 15:
            ring_copy(u, 0).start()
            ring_copy(u, 1).start()

    ring_next = [0]

    def ring_some(n):
        for _ in range(n):
            if ring_next[0] < 17:
                ring_step(ring_next[0])
                ring_next[0] += 1

    def shared_done():
        for h in (0, 1):
            blk = tgt.at[z, 1 - c, h]
            rc(blk, blk, sbs.at[h], sbr.at[h], sib).wait_recv()
        for u in range(15):
            step, up_half, dn_half = ring_at(u)
            for way in (0, 1):
                pos_z = (z + NZ - 1 - step) % NZ if way == 0 else (z + 1 + step) % NZ
                blk = tgt.at[pos_z, 1 - c, up_half if way == 0 else dn_half]
                n = 2 + 2 * u + way
                rc(blk, blk, sbs.at[n], sbr.at[n], sib).wait_recv()

    def ring_sends_done():
        for u in range(15):
            for way in (0, 1):
                ring_copy(u, way).wait_send()
                blk = ring_got(u, way)
                n = 2 + 2 * u + way
                rc(blk, blk, sbs.at[n], sbr.at[n], sib).wait_send()
        for h in (0, 1):
            blk = tgt.at[z, c, h]
            rc(blk, blk, sbs.at[h], sbr.at[h], sib).wait_send()

    stages = (gather_in, gather_mid, gather_on, work, reduce_on, reduce_b, reduce_a)

    def flow(p):
        for n, (i, ch) in enumerate(ORDER):
            stages[i](p, ch)
            if p == 0 and n >= 9:
                ring_some(1)

    put_out(0, dot(disp_b, hid[...]))
    pl.semaphore_wait(barrier, NS - 1 + 6)
    send_out(0)
    for cp in loads[5:]:
        cp.wait()
    picked_hidden = dot(pick_b, hid[...])
    win[...] = wint[...].T
    woutt[...] = wout[...].T
    flow(0)
    ring_some(17)

    lane = lax.broadcasted_iota(jnp.int32, (MK, NS * MK), 1)
    sub = lax.broadcasted_iota(jnp.int32, (MK, NS * MK), 0)
    own = jnp.where(lane == sub + s * MK, 1.0, 0.0)
    dis_f = jnp.concatenate([dis[j].astype(F32) for j in range(NEG)] + [jnp.zeros((16 - NEG, MK), F32)], axis=0).T
    lane_f = lane.astype(F32)
    count = own
    for j in range(NEG):
        count = count + jnp.where(dis_f[:, j : j + 1] == lane_f, 1.0, 0.0)
    shared_done()
    norms = []
    for q in range(NZ):
        v = tgt[q].reshape(2 * MK, D).astype(F32)
        n2 = jnp.sum(v * v, axis=1, keepdims=True)
        norms.append(jnp.broadcast_to(n2, (2 * MK, 128)).T[0:1, :])
    t_inv = 1.0 / jnp.sqrt(jnp.concatenate(norms, axis=1) + EPS)

    eout = returned(0)
    coef = (mrow_t * gate_row).T
    c_hi, c_lo = pieces(coef)
    mixed = picked_hidden + (dot(c_hi, eout) + dot(c_lo, eout))
    ctx_b = mixed.astype(BF)
    ctx = ctx_b.astype(F32)
    c_inv = 1.0 / jnp.sqrt(jnp.sum(ctx * ctx, axis=1, keepdims=True) + EPS)
    everyone = tgt[...].reshape(NS * MK, D)
    logits = dot_nt(ctx_b, everyone) * (c_inv * (1.0 / SHARP)) * t_inv
    log_total = jnp.log(jnp.sum(count * jnp.exp(logits), axis=1, keepdims=True))
    loss = log_total - jnp.sum(own * logits, axis=1, keepdims=True)
    lossv[:, :MK] = jnp.broadcast_to(loss, (MK, 128)).T[0:1, :]
    share = count * jnp.exp(logits - log_total)
    coef = (share - own) * (SCALE / SHARP) * t_inv
    c_hi, c_lo = pieces(coef)
    grad_unit = dot(c_hi, everyone) + dot(c_lo, everyone)
    ctx_unit = ctx * c_inv
    along = jnp.sum(grad_unit * ctx_unit, axis=1, keepdims=True)
    grad_ctx = (grad_unit - along * ctx_unit) * c_inv
    g_hi, g_lo = pieces(grad_ctx)
    g_two = jnp.concatenate([g_hi, g_lo], axis=0)

    mrow_b = mrow_t.astype(BF)
    grad_rows = dot(jnp.concatenate([mrow_b, mrow_b], axis=1), g_two) * gate_row
    put_out(1, grad_rows)
    send_out(1)
    q_two = dot_nt(eout, g_two)
    q_row = jnp.sum(mrow_t * (q_two[:, :MK] + q_two[:, MK:]), axis=1, keepdims=True)
    for t in (0, 1):
        ggv[t : t + 1, :] = jnp.sum(own_row[t] * q_row, axis=0, keepdims=True)
    grad_mixed = dot(jnp.concatenate([spread_b, spread_b], axis=1), g_two)
    outs = [
        pltpu.make_async_copy(lossv.at[:, pl.ds(0, 128)], loss_ref, osem.at[0]),
        pltpu.make_async_copy(ggv, gg_ref, osem.at[1]),
        pltpu.make_async_copy(dwov, dwo_ref, osem.at[2]),
        pltpu.make_async_copy(dwiv, dwi_ref, osem.at[3]),
        pltpu.make_async_copy(ghv, gh_ref, osem.at[4]),
    ]
    outs[0].start()
    outs[1].start()
    flow(1)

    grads = grp[1].reshape(16 * ROWS, D)
    for n in range(5):
        dwov[:, 256 * n : 256 * n + 256] = dot(act_t[...], grads[:, 256 * n : 256 * n + 256]).astype(BF)
    outs[2].start()
    rows = grp[0].reshape(16 * ROWS, D)
    for n in range(5):
        dwiv[:, 256 * n : 256 * n + 256] = dot(gpre_t[...], rows[:, 256 * n : 256 * n + 256]).astype(BF)
    outs[3].start()
    ghv[...] = (grad_mixed + dot(disp_t, returned(1))).astype(BF)
    outs[4].start()
    ring_sends_done()
    sends_done(0)
    sends_done(1)
    for cp in outs:
        cp.wait()


def local(
    hidden, gate_probs, expert_ids, slot_ids, mask_pos, distractors, targets, weight_in, weight_out
):
    dma = pltpu.SemaphoreType.DMA
    vm = pltpu.VMEM
    hbm = pl.BlockSpec(memory_space=pl.ANY)
    outs = pl.pallas_call(
        kernel,
        out_shape=(
            jax.ShapeDtypeStruct((1, 128), F32),
            jax.ShapeDtypeStruct((2, FR), F32),
            jax.ShapeDtypeStruct((FR, D), BF),
            jax.ShapeDtypeStruct((HID, D), BF),
            jax.ShapeDtypeStruct((HID, D), BF),
        ),
        in_specs=[hbm] * 9,
        out_specs=(hbm,) * 5,
        scratch_shapes=[
            vm((FR, D), BF),
            vm((2, FR), F32),
            vm((2, FR), jnp.int32),
            vm((2, FR), jnp.int32),
            vm((1, MK), jnp.int32),
            vm((NEG, 1, MK), jnp.int32),
            vm((D, HID), BF),
            vm((HID, D), BF),
            vm((HID, D), BF),
            vm((D, HID), BF),
            vm((NZ, 2, 2, 32, D), BF),
            vm((2, NS, 2, D), BF),
            vm((2, NS, 2, D), BF),
            vm((2, CHUNKS, 4, 4, 16, D), BF),
            vm((2, CHUNKS, 4, 4, 16, D), BF),
            vm((2, CHUNKS, 3, 4, 16, D), BF),
            vm((2, CHUNKS, 4, 16, D), BF),
            vm((2, CHUNKS, 3, 16, D), BF),
            vm((2, NS, 2, D), BF),
            vm((2, NS, 2, D), BF),
            vm((HID, 16 * ROWS), BF),
            vm((16 * ROWS, HID), F32),
            vm((HID, 16 * ROWS), BF),
            vm((1, 128), F32),
            vm((2, FR), F32),
            vm((FR, D), BF),
            vm((HID, D), BF),
            vm((HID, D), BF),
            dma((10,)),
            dma((5,)),
            dma((2, CHUNKS)),
            dma((2, CHUNKS)),
            dma((2, CHUNKS, 3)),
            dma((2, CHUNKS, 3)),
            dma((2, CHUNKS, 3)),
            dma((2, CHUNKS, 3)),
            dma((2, CHUNKS, 3)),
            dma((2, CHUNKS, 3)),
            dma((2, CHUNKS, 3)),
            dma((2, CHUNKS, 3)),
            dma((2, CHUNKS)),
            dma((2, CHUNKS)),
            dma((2, 15)),
            dma((2, 15)),
            dma((32,)),
            dma((32,)),
        ],
        compiler_params=pltpu.CompilerParams(
            collective_id=0, has_side_effects=True, vmem_limit_bytes=56 * 2**20
        ),
        cost_estimate=pl.CostEstimate(
            flops=6_000_000_000, bytes_accessed=8_000_000, transcendentals=1_000_000
        ),
        name="experts",
    )(
        hidden[0], gate_probs[0], expert_ids[0], slot_ids[0], mask_pos, jnp.swapaxes(distractors, 0, 1),
        targets[0], weight_in[0].T, weight_out[0],
    )
    loss, gate_grad, grad_hidden, grad_in, grad_out = outs
    return (loss[:, :MK], gate_grad[None], grad_hidden[None], grad_in.T[None], grad_out[None])


def solution(mesh):
    return jax.shard_map(
        local,
        mesh=mesh,
        in_specs=(
            P("dp", "seq", None),
            P("dp", None, "seq"),
            P("dp", None, "seq"),
            P("dp", None, "seq"),
            P("dp", "seq"),
            P("dp", None, "seq"),
            P("dp", "seq", None),
            P("seq", None, "dp"),
            P("seq", "dp", None),
        ),
        out_specs=(
            P("dp", "seq"),
            P("dp", None, "seq"),
            P("dp", "seq", None),
            P("seq", None, "dp"),
            P("seq", "dp", None),
        ),
        check_vma=False,
    )
```

```python
import jax
import jax.numpy as jnp
from jax import lax
from jax.experimental import pallas as pl
from jax.experimental.pallas import tpu as pltpu
from jax.sharding import PartitionSpec as P

MESH = pl.DeviceIdType.MESH
BF = jnp.bfloat16
F32 = jnp.float32
NZ = 16
NS = 32
CHUNKS = 4
D = 1280
HID = 320
ROWS = 64
FR = 128
MK = 64
NEG = 10
EPS = 1e-06
SHARP = 0.1
SCALE = 64.0
ORDER = [
    (0, 0), (0, 1), (1, 0), (0, 2), (1, 1), (2, 0), (0, 3), (1, 2), (2, 1), (1, 3), (3, 0), (2, 2),
    (2, 3), (3, 1), (3, 2), (3, 3), (4, 0), (4, 1), (4, 2), (4, 3), (5, 0), (5, 1), (5, 2), (5, 3),
    (6, 0), (6, 1), (6, 2), (6, 3),
]
FAR = (0, 3, 1, 2)
DZ = [0] + [(h + 1) // 2 if h % 2 else NZ - h // 2 for h in range(1, NZ)]


def dot(a, b):
    return jnp.dot(a, b, preferred_element_type=F32)


def dot_nt(a, b):
    return lax.dot_general(a, b, (((1,), (1,)), ((), ())), preferred_element_type=F32)


def pieces(v):
    hi = v.astype(BF)
    lo = (v - hi.astype(F32)).astype(BF)
    return hi, lo


def gelu_parts(x):
    k = 0.7978845608028654
    x2 = x * x
    t = jnp.tanh(k * (x + 0.044715 * (x2 * x)))
    half = 0.5 * (1.0 + t)
    slope = half + 0.5 * x * (1.0 - t * t) * (k * (1.0 + (3 * 0.044715) * x2))
    return x * half, slope


def kernel(
    hid_ref, gate_ref, exp_ref, slot_ref, pos_ref, dis_ref, tgt_ref, win_ref, wout_ref,
    loss_ref, gg_ref, gh_ref, dwi_ref, dwo_ref,
    hid, gate, exps, slots, pos, dis, win, wout, wint, woutt,
    tgt, out, inn, grp, part, rsb, acc, rsa, rout, ret,
    act_t, slope, gpre_t, lossv, ggv, ghv, dwiv, dwov,
    lsem, osem,
    ds, dr, gas, gar, gbs, gbr, bs, br, as_, ar, ts, tr,
    rgs, rgr, sbs, sbr,
):
    dp, s = lax.axis_index("dp"), lax.axis_index("seq")
    z, c = s // 2, s % 2
    y, x = dp // 4, dp % 4
    a = x + c * (y - x)
    b = y + c * (x - y)

    def dpi(aa, bb):
        return aa * (1 + 3 * c) + bb * (4 - 3 * c)

    apeer = {d: (dpi((a + d) % 4, b), s) for d in (1, 2, 3)}
    bpeer = {d: (dpi(a, (b + d) % 4), s) for d in (1, 2, 3)}

    def zpeer(k):
        return (dp, ((z + NZ - DZ[k // 2]) % NZ) * 2 + (c + k % 2) % 2)

    def zback(k):
        return (dp, ((z + DZ[k // 2]) % NZ) * 2 + (c + k % 2) % 2)

    zup = (dp, ((z + 1) % NZ) * 2 + c)
    zdn = (dp, ((z + NZ - 1) % NZ) * 2 + c)
    sib = (dp, z * 2 + 1 - c)

    def rc(src, dst, ssem, rsem, dev):
        return pltpu.make_async_remote_copy(
            src_ref=src, dst_ref=dst, send_sem=ssem, recv_sem=rsem, device_id=dev, device_id_type=MESH
        )

    loads = [
        (hid_ref, hid), (gate_ref, gate), (exp_ref, exps), (slot_ref, slots), (pos_ref, pos),
        (dis_ref, dis), (win_ref, wint), (wout_ref, wout),
    ]
    loads = [pltpu.make_async_copy(p, q, lsem.at[i]) for i, (p, q) in enumerate(loads)]
    tloads = [
        pltpu.make_async_copy(tgt_ref.at[pl.ds(32 * h, 32)], tgt.at[z, c, h], lsem.at[len(loads) + h])
        for h in (0, 1)
    ]
    for cp in loads + tloads:
        cp.start()
    barrier = pltpu.get_barrier_semaphore()
    for k in range(1, NS):
        pl.semaphore_signal(barrier, inc=1, device_id=zpeer(k), device_id_type=MESH)
    for d in (1, 2, 3):
        pl.semaphore_signal(barrier, inc=1, device_id=apeer[d], device_id_type=MESH)
        pl.semaphore_signal(barrier, inc=1, device_id=bpeer[d], device_id_type=MESH)

    for cp in loads[:5]:
        cp.wait()

    row = lax.broadcasted_iota(jnp.int32, (ROWS, FR), 0)
    kk = row >> 1
    hh = kk >> 1
    dz = jnp.where((hh & 1) == 1, (hh + 1) >> 1, (NZ - (hh >> 1)) & (NZ - 1))
    want = (((z + NZ - dz) & (NZ - 1)) << 1) + ((c + (kk & 1)) & 1)
    cap = row & 1
    own_row = [
        jnp.where((exps[t : t + 1, :] == want) & (slots[t : t + 1, :] == cap), 1.0, 0.0) for t in (0, 1)
    ]
    disp = own_row[0] + own_row[1]
    disp_b = disp.astype(BF)

    def put_out(p, rows):
        for k in range(NS):
            out[p, k] = rows[2 * k : 2 * k + 2].astype(BF)

    def send_out(p):
        for k in range(1, NS):
            rc(out.at[p, k], inn.at[p, k], ds.at[p, k // 8], dr.at[p, k // 8], zpeer(k)).start()
        inn[p, 0] = out[p, 0]

    def span(ch):
        return pl.ds(8 * ch, 8) if ch else pl.ds(1, 7)

    def gather_in(p, ch):
        rc(out.at[p, span(ch)], inn.at[p, span(ch)], ds.at[p, ch], dr.at[p, ch], zup).wait_recv()
        rows = inn[p, 8 * ch : 8 * ch + 8].astype(F32).reshape(16, D).astype(BF)
        grp[p, b, ch, a] = rows
        blk = grp.at[p, b, ch, a]
        for d in (1, 2, 3):
            rc(blk, blk, gas.at[p, ch, d - 1], gar.at[p, ch, d - 1], apeer[d]).start()

    def gather_mid(p, ch):
        for d in (1, 2, 3):
            blk = grp.at[p, b, ch, (a + 4 - d) % 4]
            rc(blk, blk, gas.at[p, ch, d - 1], gar.at[p, ch, d - 1], apeer[d]).wait_recv()
        for slot in (0, 1):
            b_copy(p, ch, slot).start()

    def fore(ch):
        return 1 if ch % 2 == 0 else 3

    def b_copy(p, ch, slot):
        g = fore(ch)
        blk = grp.at[p, (b + 4 - g) % 4, ch] if slot == 2 else grp.at[p, b, ch]
        dev = bpeer[4 - g] if slot == 1 else bpeer[g]
        return rc(blk, blk, gbs.at[p, ch, slot], gbr.at[p, ch, slot], dev)

    def b_wait(p, ch, slot):
        g = fore(ch)
        blk = grp.at[p, (b + (4 - g, g, 2)[slot]) % 4, ch]
        rc(blk, blk, gbs.at[p, ch, slot], gbr.at[p, ch, slot], bpeer[g]).wait_recv()

    def gather_on(p, ch):
        b_wait(p, ch, 0)
        b_copy(p, ch, 2).start()

    def sum_copy(p, ch, slot):
        g = fore(ch)
        blk = part.at[p, (b + (2, 4 - g, g)[slot]) % 4, ch]
        dev = bpeer[4 - g] if slot == 1 else bpeer[g]
        return rc(blk, rsb.at[p, ch, slot], bs.at[p, ch, slot], br.at[p, ch, slot], dev)

    def work(p, u):
        d = FAR[u]
        at = (b + d) % 4
        for ch in range(CHUNKS):
            if d == 2:
                b_wait(p, ch, 2)
            elif d == fore(ch):
                b_wait(p, ch, 1)
        rows = grp[p, at].reshape(256, D)
        if p == 0:
            act, slp = gelu_parts(dot(rows, win[...]))
            act = act.astype(BF)
            part[p, at] = dot(act, wout[...]).astype(BF).reshape(CHUNKS, 4, 16, D)
        else:
            grad_pre = (dot(rows, woutt[...]) * slope[at]).astype(BF)
            part[p, at] = dot(grad_pre, wint[...]).astype(BF).reshape(CHUNKS, 4, 16, D)
        for ch in range(CHUNKS):
            if d == 2:
                sum_copy(p, ch, 0).start()
            elif d == 4 - fore(ch):
                sum_copy(p, ch, 1).start()
        if p == 0:
            slope[at] = slp
            act_t[at] = act.T
        else:
            gpre_t[at] = grad_pre.T

    def reduce_on(p, ch):
        nxt = (b + fore(ch)) % 4
        sum_copy(p, ch, 0).wait_recv()
        part[p, nxt, ch] = (part[p, nxt, ch].astype(F32) + rsb[p, ch, 0].astype(F32)).astype(BF)
        sum_copy(p, ch, 2).start()

    def reduce_b(p, ch):
        sum_copy(p, ch, 1).wait_recv()
        sum_copy(p, ch, 2).wait_recv()
        total = part[p, b, ch].astype(F32) + (rsb[p, ch, 1].astype(F32) + rsb[p, ch, 2].astype(F32))
        acc[p, ch] = total.astype(BF)
        for d in (1, 2, 3):
            rc(
                acc.at[p, ch, (a + d) % 4], rsa.at[p, ch, d - 1], as_.at[p, ch, d - 1], ar.at[p, ch, d - 1],
                apeer[d],
            ).start()

    def reduce_a(p, ch):
        for d in (1, 2, 3):
            rc(
                acc.at[p, ch, (a + d) % 4], rsa.at[p, ch, d - 1], as_.at[p, ch, d - 1], ar.at[p, ch, d - 1],
                apeer[d],
            ).wait_recv()
        total = (acc[p, ch, a].astype(F32) + rsa[p, ch, 0].astype(F32)) + (
            rsa[p, ch, 1].astype(F32) + rsa[p, ch, 2].astype(F32)
        )
        rout[p, 8 * ch : 8 * ch + 8] = total.reshape(8, 2, D).astype(BF)
        for k in range(8 * ch, 8 * ch + 8):
            if k:
                rc(rout.at[p, k], ret.at[p, k], ts.at[p, ch], tr.at[p, ch], zback(k)).start()
        if ch == 0:
            ret[p, 0] = rout[p, 0]

    def returned(p):
        for ch in range(CHUNKS):
            rc(rout.at[p, span(ch)], ret.at[p, span(ch)], ts.at[p, ch], tr.at[p, ch], zup).wait_recv()
        return ret[p].astype(F32).reshape(ROWS, D).astype(BF)

    def sends_done(p):
        for ch in range(CHUNKS):
            rc(out.at[p, span(ch)], inn.at[p, span(ch)], ds.at[p, ch], dr.at[p, ch], zup).wait_send()
            rc(rout.at[p, span(ch)], ret.at[p, span(ch)], ts.at[p, ch], tr.at[p, ch], zup).wait_send()
            for d in (1, 2, 3):
                blk = grp.at[p, b, ch, a]
                rc(blk, blk, gas.at[p, ch, d - 1], gar.at[p, ch, d - 1], apeer[d]).wait_send()
                b_copy(p, ch, d - 1).wait_send()
                sum_copy(p, ch, d - 1).wait_send()
                rc(
                    acc.at[p, ch, (a + d) % 4], rsa.at[p, ch, d - 1], as_.at[p, ch, d - 1],
                    ar.at[p, ch, d - 1], apeer[d],
                ).wait_send()

    def ring_at(u):
        step, half = u // 2, u % 2
        up_half = half if u < 14 else 0
        dn_half = half if u < 14 else 1
        return step, up_half, dn_half

    def ring_copy(u, way):
        step, up_half, dn_half = ring_at(u)
        if way == 0:
            blk = tgt.at[(z + NZ - step) % NZ, c, up_half]
            return rc(blk, blk, rgs.at[0, u], rgr.at[0, u], zup)
        blk = tgt.at[(z + step) % NZ, c, dn_half]
        return rc(blk, blk, rgs.at[1, u], rgr.at[1, u], zdn)

    def ring_got(u, way):
        step, up_half, dn_half = ring_at(u)
        if way == 0:
            return tgt.at[(z + NZ - 1 - step) % NZ, c, up_half]
        return tgt.at[(z + 1 + step) % NZ, c, dn_half]

    def ring_take(u):
        for way in (0, 1):
            blk = ring_got(u, way)
            rc(blk, blk, rgs.at[way, u], rgr.at[way, u], zup).wait_recv()
            n = 2 + 2 * u + way
            rc(blk, blk, sbs.at[n], sbr.at[n], sib).start()

    def ring_step(u):
        if u == 0:
            for h in (0, 1):
                tloads[h].wait()
                blk = tgt.at[z, c, h]
                rc(blk, blk, sbs.at[h], sbr.at[h], sib).start()
        if 2 <= u != 15:
            ring_take(u - 2)
        if u == 14:
            ring_take(13)
        if u < 15:
            ring_copy(u, 0).start()
            ring_copy(u, 1).start()

    ring_next = [0]

    def ring_some(n):
        for _ in range(n):
            if ring_next[0] < 17:
                ring_step(ring_next[0])
                ring_next[0] += 1

    def shared_done():
        for h in (0, 1):
            blk = tgt.at[z, 1 - c, h]
            rc(blk, blk, sbs.at[h], sbr.at[h], sib).wait_recv()
        for u in range(15):
            step, up_half, dn_half = ring_at(u)
            for way in (0, 1):
                pos_z = (z + NZ - 1 - step) % NZ if way == 0 else (z + 1 + step) % NZ
                blk = tgt.at[pos_z, 1 - c, up_half if way == 0 else dn_half]
                n = 2 + 2 * u + way
                rc(blk, blk, sbs.at[n], sbr.at[n], sib).wait_recv()

    def ring_sends_done():
        for u in range(15):
            for way in (0, 1):
                ring_copy(u, way).wait_send()
                blk = ring_got(u, way)
                n = 2 + 2 * u + way
                rc(blk, blk, sbs.at[n], sbr.at[n], sib).wait_send()
        for h in (0, 1):
            blk = tgt.at[z, c, h]
            rc(blk, blk, sbs.at[h], sbr.at[h], sib).wait_send()

    stages = (gather_in, gather_mid, gather_on, work, reduce_on, reduce_b, reduce_a)

    def flow(p):
        for n, (i, ch) in enumerate(ORDER):
            stages[i](p, ch)
            if p == 0 and n >= 9:
                ring_some(1)

    put_out(0, dot(disp_b, hid[...]))
    pl.semaphore_wait(barrier, NS - 1 + 6)
    send_out(0)
    gate_row = jnp.sum(
        own_row[0] * gate[0:1, :] + own_row[1] * gate[1:2, :], axis=1, keepdims=True
    )
    disp_t = disp.T.astype(BF)
    spread = jnp.where(lax.broadcasted_iota(jnp.int32, (FR, MK), 0) == pos[0:1, :], 1.0, 0.0)
    spread_b = spread.astype(BF)
    pick_b = spread.T.astype(BF)
    mrow_t = dot(disp_b, spread_b)
    for cp in loads[5:]:
        cp.wait()
    picked_hidden = dot(pick_b, hid[...])
    win[...] = wint[...].T
    woutt[...] = wout[...].T
    flow(0)
    ring_some(17)

    lane = lax.broadcasted_iota(jnp.int32, (MK, NS * MK), 1)
    sub = lax.broadcasted_iota(jnp.int32, (MK, NS * MK), 0)
    own = jnp.where(lane == sub + s * MK, 1.0, 0.0)
    dis_f = jnp.concatenate([dis[j].astype(F32) for j in range(NEG)] + [jnp.zeros((16 - NEG, MK), F32)], axis=0).T
    lane_f = lane.astype(F32)
    count = own
    for j in range(NEG):
        count = count + jnp.where(dis_f[:, j : j + 1] == lane_f, 1.0, 0.0)
    shared_done()
    norms = []
    for q in range(NZ):
        v = tgt[q].reshape(2 * MK, D).astype(F32)
        n2 = jnp.sum(v * v, axis=1, keepdims=True)
        norms.append(jnp.broadcast_to(n2, (2 * MK, 128)).T[0:1, :])
    t_inv = 1.0 / jnp.sqrt(jnp.concatenate(norms, axis=1) + EPS)

    eout = returned(0)
    coef = (mrow_t * gate_row).T
    c_hi, c_lo = pieces(coef)
    mixed = picked_hidden + (dot(c_hi, eout) + dot(c_lo, eout))
    ctx_b = mixed.astype(BF)
    ctx = ctx_b.astype(F32)
    c_inv = 1.0 / jnp.sqrt(jnp.sum(ctx * ctx, axis=1, keepdims=True) + EPS)
    everyone = tgt[...].reshape(NS * MK, D)
    logits = dot_nt(ctx_b, everyone) * (c_inv * (1.0 / SHARP)) * t_inv
    log_total = jnp.log(jnp.sum(count * jnp.exp(logits), axis=1, keepdims=True))
    loss = log_total - jnp.sum(own * logits, axis=1, keepdims=True)
    lossv[:, :MK] = jnp.broadcast_to(loss, (MK, 128)).T[0:1, :]
    share = count * jnp.exp(logits - log_total)
    coef = (share - own) * (SCALE / SHARP) * t_inv
    c_hi, c_lo = pieces(coef)
    grad_unit = dot(c_hi, everyone) + dot(c_lo, everyone)
    ctx_unit = ctx * c_inv
    along = jnp.sum(grad_unit * ctx_unit, axis=1, keepdims=True)
    grad_ctx = (grad_unit - along * ctx_unit) * c_inv
    g_hi, g_lo = pieces(grad_ctx)
    g_two = jnp.concatenate([g_hi, g_lo], axis=0)

    mrow_b = mrow_t.astype(BF)
    grad_rows = dot(jnp.concatenate([mrow_b, mrow_b], axis=1), g_two) * gate_row
    put_out(1, grad_rows)
    send_out(1)
    q_two = dot_nt(eout, g_two)
    q_row = jnp.sum(mrow_t * (q_two[:, :MK] + q_two[:, MK:]), axis=1, keepdims=True)
    for t in (0, 1):
        ggv[t : t + 1, :] = jnp.sum(own_row[t] * q_row, axis=0, keepdims=True)
    grad_mixed = dot(jnp.concatenate([spread_b, spread_b], axis=1), g_two)
    outs = [
        pltpu.make_async_copy(lossv.at[:, pl.ds(0, 128)], loss_ref, osem.at[0]),
        pltpu.make_async_copy(ggv, gg_ref, osem.at[1]),
        pltpu.make_async_copy(dwov, dwo_ref, osem.at[2]),
        pltpu.make_async_copy(dwiv, dwi_ref, osem.at[3]),
        pltpu.make_async_copy(ghv, gh_ref, osem.at[4]),
    ]
    outs[0].start()
    outs[1].start()
    flow(1)

    def over_rows(left, right, n):
        total = dot(left[0], right[0, :, 256 * n : 256 * n + 256])
        for g in range(1, 4):
            total = total + dot(left[g], right[g, :, 256 * n : 256 * n + 256])
        return total.astype(BF)

    rows = grp[1].reshape(4, 4 * ROWS, D)
    for n in range(5):
        dwov[:, 256 * n : 256 * n + 256] = over_rows(act_t, rows, n)
    outs[2].start()
    rows = grp[0].reshape(4, 4 * ROWS, D)
    for n in range(5):
        dwiv[:, 256 * n : 256 * n + 256] = over_rows(gpre_t, rows, n)
    outs[3].start()
    ghv[...] = (grad_mixed + dot(disp_t, returned(1))).astype(BF)
    outs[4].start()
    ring_sends_done()
    sends_done(0)
    sends_done(1)
    for cp in outs:
        cp.wait()


def local(
    hidden, gate_probs, expert_ids, slot_ids, mask_pos, distractors, targets, weight_in, weight_out
):
    dma = pltpu.SemaphoreType.DMA
    vm = pltpu.VMEM
    hbm = pl.BlockSpec(memory_space=pl.ANY)
    outs = pl.pallas_call(
        kernel,
        out_shape=(
            jax.ShapeDtypeStruct((1, 128), F32),
            jax.ShapeDtypeStruct((2, FR), F32),
            jax.ShapeDtypeStruct((FR, D), BF),
            jax.ShapeDtypeStruct((HID, D), BF),
            jax.ShapeDtypeStruct((HID, D), BF),
        ),
        in_specs=[hbm] * 9,
        out_specs=(hbm,) * 5,
        scratch_shapes=[
            vm((FR, D), BF),
            vm((2, FR), F32),
            vm((2, FR), jnp.int32),
            vm((2, FR), jnp.int32),
            vm((1, MK), jnp.int32),
            vm((NEG, 1, MK), jnp.int32),
            vm((D, HID), BF),
            vm((HID, D), BF),
            vm((HID, D), BF),
            vm((D, HID), BF),
            vm((NZ, 2, 2, 32, D), BF),
            vm((2, NS, 2, D), BF),
            vm((2, NS, 2, D), BF),
            vm((2, CHUNKS, 4, 4, 16, D), BF),
            vm((2, CHUNKS, 4, 4, 16, D), BF),
            vm((2, CHUNKS, 3, 4, 16, D), BF),
            vm((2, CHUNKS, 4, 16, D), BF),
            vm((2, CHUNKS, 3, 16, D), BF),
            vm((2, NS, 2, D), BF),
            vm((2, NS, 2, D), BF),
            vm((4, HID, 4 * ROWS), BF),
            vm((4, 4 * ROWS, HID), F32),
            vm((4, HID, 4 * ROWS), BF),
            vm((1, 128), F32),
            vm((2, FR), F32),
            vm((FR, D), BF),
            vm((HID, D), BF),
            vm((HID, D), BF),
            dma((10,)),
            dma((5,)),
            dma((2, CHUNKS)),
            dma((2, CHUNKS)),
            dma((2, CHUNKS, 3)),
            dma((2, CHUNKS, 3)),
            dma((2, CHUNKS, 3)),
            dma((2, CHUNKS, 3)),
            dma((2, CHUNKS, 3)),
            dma((2, CHUNKS, 3)),
            dma((2, CHUNKS, 3)),
            dma((2, CHUNKS, 3)),
            dma((2, CHUNKS)),
            dma((2, CHUNKS)),
            dma((2, 15)),
            dma((2, 15)),
            dma((32,)),
            dma((32,)),
        ],
        compiler_params=pltpu.CompilerParams(
            collective_id=0, has_side_effects=True, vmem_limit_bytes=56 * 2**20
        ),
        cost_estimate=pl.CostEstimate(
            flops=6_000_000_000, bytes_accessed=8_000_000, transcendentals=1_000_000
        ),
        name="experts",
    )(
        hidden[0], gate_probs[0], expert_ids[0], slot_ids[0], mask_pos, jnp.swapaxes(distractors, 0, 1),
        targets[0], weight_in[0].T, weight_out[0],
    )
    loss, gate_grad, grad_hidden, grad_in, grad_out = outs
    return (loss[:, :MK], gate_grad[None], grad_hidden[None], grad_in.T[None], grad_out[None])


def solution(mesh):
    return jax.shard_map(
        local,
        mesh=mesh,
        in_specs=(
            P("dp", "seq", None),
            P("dp", None, "seq"),
            P("dp", None, "seq"),
            P("dp", None, "seq"),
            P("dp", "seq"),
            P("dp", None, "seq"),
            P("dp", "seq", None),
            P("seq", None, "dp"),
            P("seq", "dp", None),
        ),
        out_specs=(
            P("dp", "seq"),
            P("dp", None, "seq"),
            P("dp", "seq", None),
            P("seq", None, "dp"),
            P("seq", "dp", None),
        ),
        check_vma=False,
    )
```

```python
import jax
import jax.numpy as jnp
from jax import lax
from jax.experimental import pallas as pl
from jax.experimental.pallas import tpu as pltpu
from jax.sharding import PartitionSpec as P

MESH = pl.DeviceIdType.MESH
BF = jnp.bfloat16
F32 = jnp.float32
NZ = 16
NS = 32
CHUNKS = 4
D = 1280
HID = 320
ROWS = 64
FR = 128
MK = 64
NEG = 10
EPS = 1e-06
SHARP = 0.1
SCALE = 64.0
ORDER = [
    (0, 0), (0, 1), (1, 0), (0, 2), (1, 1), (2, 0), (0, 3), (1, 2), (2, 1), (1, 3), (2, 2), (3, 0),
    (2, 3), (3, 1), (3, 2), (3, 3), (4, 0), (4, 1), (4, 2), (4, 3), (5, 0), (5, 1), (5, 2), (5, 3),
    (6, 0), (6, 1), (6, 2), (6, 3),
]
RING_AT = (4, 6, 8, 10, 11, 12, 13, 14, 15, 17, 19, 21, 23, 25, 27)
DZ = [0] + [(h + 1) // 2 if h % 2 else NZ - h // 2 for h in range(1, NZ)]


def dot(a, b):
    return jnp.dot(a, b, preferred_element_type=F32)


def dot_nt(a, b):
    return lax.dot_general(a, b, (((1,), (1,)), ((), ())), preferred_element_type=F32)


def pieces(v):
    hi = v.astype(BF)
    lo = (v - hi.astype(F32)).astype(BF)
    return hi, lo


def gelu_parts(x):
    k = 0.7978845608028654
    x2 = x * x
    t = jnp.tanh(k * (x + 0.044715 * (x2 * x)))
    half = 0.5 * (1.0 + t)
    slope = half + 0.5 * x * (1.0 - t * t) * (k * (1.0 + (3 * 0.044715) * x2))
    return x * half, slope


def kernel(
    hid_ref, gate_ref, exp_ref, slot_ref, pos_ref, dis_ref, tgt_ref, win_ref, wout_ref,
    loss_ref, gg_ref, gh_ref, dwi_ref, dwo_ref,
    hid, gate, exps, slots, pos, dis, win, wout, wint, woutt,
    tgt, out, inn, grp, part, rsb, acc, rsa, rout, ret,
    act_t, slope, gpre_t, chosen, lossv, ggv, ghv, dwiv, dwov,
    lsem, osem,
    ds, dr, gas, gar, gbs, gbr, bs, br, as_, ar, ts, tr,
    rgs, rgr, sbs, sbr,
):
    dp, s = lax.axis_index("dp"), lax.axis_index("seq")
    z, c = s // 2, s % 2
    y, x = dp // 4, dp % 4
    a = x + c * (y - x)
    b = y + c * (x - y)

    def dpi(aa, bb):
        return aa * (1 + 3 * c) + bb * (4 - 3 * c)

    apeer = {d: (dpi((a + d) % 4, b), s) for d in (1, 2, 3)}
    bpeer = {d: (dpi(a, (b + d) % 4), s) for d in (1, 2, 3)}

    def zpeer(k):
        return (dp, ((z + NZ - DZ[k // 2]) % NZ) * 2 + (c + k % 2) % 2)

    def zback(k):
        return (dp, ((z + DZ[k // 2]) % NZ) * 2 + (c + k % 2) % 2)

    zup = (dp, ((z + 1) % NZ) * 2 + c)
    zdn = (dp, ((z + NZ - 1) % NZ) * 2 + c)
    sib = (dp, z * 2 + 1 - c)

    def rc(src, dst, ssem, rsem, dev):
        return pltpu.make_async_remote_copy(
            src_ref=src, dst_ref=dst, send_sem=ssem, recv_sem=rsem, device_id=dev, device_id_type=MESH
        )

    loads = [
        (hid_ref, hid), (gate_ref, gate), (exp_ref, exps), (slot_ref, slots), (pos_ref, pos),
        (dis_ref, dis), (win_ref, wint), (wout_ref, wout),
    ]
    loads = [pltpu.make_async_copy(p, q, lsem.at[i]) for i, (p, q) in enumerate(loads)]
    tloads = [
        pltpu.make_async_copy(tgt_ref.at[pl.ds(32 * h, 32)], tgt.at[z, c, h], lsem.at[len(loads) + h])
        for h in (0, 1)
    ]
    for cp in loads + tloads:
        cp.start()
    barrier = pltpu.get_barrier_semaphore()
    for k in range(1, NS):
        pl.semaphore_signal(barrier, inc=1, device_id=zpeer(k), device_id_type=MESH)
    for d in (1, 2, 3):
        pl.semaphore_signal(barrier, inc=1, device_id=apeer[d], device_id_type=MESH)
        pl.semaphore_signal(barrier, inc=1, device_id=bpeer[d], device_id_type=MESH)

    for cp in loads[:5]:
        cp.wait()

    row = lax.broadcasted_iota(jnp.int32, (ROWS, FR), 0)
    kk = row >> 1
    hh = kk >> 1
    dz = jnp.where((hh & 1) == 1, (hh + 1) >> 1, (NZ - (hh >> 1)) & (NZ - 1))
    want = (((z + NZ - dz) & (NZ - 1)) << 1) + ((c + (kk & 1)) & 1)
    cap = row & 1
    own_row = [
        jnp.where((exps[t : t + 1, :] == want) & (slots[t : t + 1, :] == cap), 1.0, 0.0) for t in (0, 1)
    ]
    disp = own_row[0] + own_row[1]
    disp_b = disp.astype(BF)

    def put_out(p, rows):
        for k in range(NS):
            out[p, k] = rows[2 * k : 2 * k + 2].astype(BF)

    def send_out(p):
        for k in range(1, NS):
            rc(out.at[p, k], inn.at[p, k], ds.at[p, k // 8], dr.at[p, k // 8], zpeer(k)).start()
        inn[p, 0] = out[p, 0]

    def span(ch):
        return pl.ds(8 * ch, 8) if ch else pl.ds(1, 7)

    def gather_in(p, ch):
        rc(out.at[p, span(ch)], inn.at[p, span(ch)], ds.at[p, ch], dr.at[p, ch], zup).wait_recv()
        rows = inn[p, 8 * ch : 8 * ch + 8].astype(F32).reshape(16, D).astype(BF)
        grp[p, ch, b, a] = rows
        blk = grp.at[p, ch, b, a]
        for d in (1, 2, 3):
            rc(blk, blk, gas.at[p, ch, d - 1], gar.at[p, ch, d - 1], apeer[d]).start()

    def gather_mid(p, ch):
        for d in (1, 2, 3):
            blk = grp.at[p, ch, b, (a + 4 - d) % 4]
            rc(blk, blk, gas.at[p, ch, d - 1], gar.at[p, ch, d - 1], apeer[d]).wait_recv()
        for slot in (0, 1):
            b_copy(p, ch, slot).start()

    def fore(ch):
        return 1 if ch % 2 == 0 else 3

    def b_copy(p, ch, slot):
        g = fore(ch)
        blk = grp.at[p, ch, (b + 4 - g) % 4] if slot == 2 else grp.at[p, ch, b]
        dev = bpeer[4 - g] if slot == 1 else bpeer[g]
        return rc(blk, blk, gbs.at[p, ch, slot], gbr.at[p, ch, slot], dev)

    def b_wait(p, ch, slot):
        g = fore(ch)
        blk = grp.at[p, ch, (b + (4 - g, g, 2)[slot]) % 4]
        rc(blk, blk, gbs.at[p, ch, slot], gbr.at[p, ch, slot], bpeer[g]).wait_recv()

    def gather_on(p, ch):
        b_wait(p, ch, 0)
        b_copy(p, ch, 2).start()

    def sum_copy(p, ch, slot):
        g = fore(ch)
        blk = part.at[p, ch, (b + (2, 4 - g, g)[slot]) % 4]
        dev = bpeer[4 - g] if slot == 1 else bpeer[g]
        return rc(blk, rsb.at[p, ch, slot], bs.at[p, ch, slot], br.at[p, ch, slot], dev)

    def work(p, ch):
        b_wait(p, ch, 1)
        b_wait(p, ch, 2)
        rows = grp[p, ch].reshape(256, D)
        if p == 0:
            act, slp = gelu_parts(dot(rows, win[...]))
            act = act.astype(BF)
            part[p, ch] = dot(act, wout[...]).astype(BF).reshape(4, 4, 16, D)
        else:
            grad_pre = (dot(rows, woutt[...]) * slope[pl.ds(256 * ch, 256), :]).astype(BF)
            part[p, ch] = dot(grad_pre, wint[...]).astype(BF).reshape(4, 4, 16, D)
        sum_copy(p, ch, 0).start()
        sum_copy(p, ch, 1).start()
        if p == 0:
            slope[pl.ds(256 * ch, 256), :] = slp
            act_t[:, 256 * ch : 256 * ch + 256] = act.T
        else:
            gpre_t[:, 256 * ch : 256 * ch + 256] = grad_pre.T

    def reduce_on(p, ch):
        nxt = (b + fore(ch)) % 4
        sum_copy(p, ch, 0).wait_recv()
        part[p, ch, nxt] = (part[p, ch, nxt].astype(F32) + rsb[p, ch, 0].astype(F32)).astype(BF)
        sum_copy(p, ch, 2).start()

    def reduce_b(p, ch):
        sum_copy(p, ch, 1).wait_recv()
        sum_copy(p, ch, 2).wait_recv()
        total = part[p, ch, b].astype(F32) + (rsb[p, ch, 1].astype(F32) + rsb[p, ch, 2].astype(F32))
        acc[p, ch] = total.astype(BF)
        for d in (1, 2, 3):
            rc(
                acc.at[p, ch, (a + d) % 4], rsa.at[p, ch, d - 1], as_.at[p, ch, d - 1], ar.at[p, ch, d - 1],
                apeer[d],
            ).start()

    def reduce_a(p, ch):
        for d in (1, 2, 3):
            rc(
                acc.at[p, ch, (a + d) % 4], rsa.at[p, ch, d - 1], as_.at[p, ch, d - 1], ar.at[p, ch, d - 1],
                apeer[d],
            ).wait_recv()
        total = (acc[p, ch, a].astype(F32) + rsa[p, ch, 0].astype(F32)) + (
            rsa[p, ch, 1].astype(F32) + rsa[p, ch, 2].astype(F32)
        )
        rout[p, 8 * ch : 8 * ch + 8] = total.reshape(8, 2, D).astype(BF)
        for k in range(8 * ch, 8 * ch + 8):
            if k:
                rc(rout.at[p, k], ret.at[p, k], ts.at[p, ch], tr.at[p, ch], zback(k)).start()
        if ch == 0:
            ret[p, 0] = rout[p, 0]

    def returned(p):
        for ch in range(CHUNKS):
            rc(rout.at[p, span(ch)], ret.at[p, span(ch)], ts.at[p, ch], tr.at[p, ch], zup).wait_recv()
        return ret[p].astype(F32).reshape(ROWS, D).astype(BF)

    def sends_done(p):
        for ch in range(CHUNKS):
            rc(out.at[p, span(ch)], inn.at[p, span(ch)], ds.at[p, ch], dr.at[p, ch], zup).wait_send()
            rc(rout.at[p, span(ch)], ret.at[p, span(ch)], ts.at[p, ch], tr.at[p, ch], zup).wait_send()
            for d in (1, 2, 3):
                blk = grp.at[p, ch, b, a]
                rc(blk, blk, gas.at[p, ch, d - 1], gar.at[p, ch, d - 1], apeer[d]).wait_send()
                b_copy(p, ch, d - 1).wait_send()
                sum_copy(p, ch, d - 1).wait_send()
                rc(
                    acc.at[p, ch, (a + d) % 4], rsa.at[p, ch, d - 1], as_.at[p, ch, d - 1],
                    ar.at[p, ch, d - 1], apeer[d],
                ).wait_send()

    def ring_at(u):
        step, half = u // 2, u % 2
        up_half = half if u < 14 else 0
        dn_half = half if u < 14 else 1
        return step, up_half, dn_half

    def ring_copy(u, way):
        step, up_half, dn_half = ring_at(u)
        if way == 0:
            blk = tgt.at[(z + NZ - step) % NZ, c, up_half]
            return rc(blk, blk, rgs.at[0, u], rgr.at[0, u], zup)
        blk = tgt.at[(z + step) % NZ, c, dn_half]
        return rc(blk, blk, rgs.at[1, u], rgr.at[1, u], zdn)

    def ring_got(u, way):
        step, up_half, dn_half = ring_at(u)
        if way == 0:
            return tgt.at[(z + NZ - 1 - step) % NZ, c, up_half]
        return tgt.at[(z + 1 + step) % NZ, c, dn_half]

    def ring_take(u):
        for way in (0, 1):
            blk = ring_got(u, way)
            rc(blk, blk, rgs.at[way, u], rgr.at[way, u], zup).wait_recv()
            n = 2 + 2 * u + way
            rc(blk, blk, sbs.at[n], sbr.at[n], sib).start()

    def ring_step(u):
        if u == 0:
            for h in (0, 1):
                tloads[h].wait()
                blk = tgt.at[z, c, h]
                rc(blk, blk, sbs.at[h], sbr.at[h], sib).start()
        if 2 <= u != 15:
            ring_take(u - 2)
        if u == 14:
            ring_take(13)
        if u < 15:
            ring_copy(u, 0).start()
            ring_copy(u, 1).start()

    ring_next = [0]

    def ring_some(n):
        for _ in range(n):
            if ring_next[0] < 17:
                ring_step(ring_next[0])
                ring_next[0] += 1

    def shared_done():
        for h in (0, 1):
            blk = tgt.at[z, 1 - c, h]
            rc(blk, blk, sbs.at[h], sbr.at[h], sib).wait_recv()
        for u in range(15):
            step, up_half, dn_half = ring_at(u)
            for way in (0, 1):
                pos_z = (z + NZ - 1 - step) % NZ if way == 0 else (z + 1 + step) % NZ
                blk = tgt.at[pos_z, 1 - c, up_half if way == 0 else dn_half]
                n = 2 + 2 * u + way
                rc(blk, blk, sbs.at[n], sbr.at[n], sib).wait_recv()

    def ring_sends_done():
        for u in range(15):
            for way in (0, 1):
                ring_copy(u, way).wait_send()
                blk = ring_got(u, way)
                n = 2 + 2 * u + way
                rc(blk, blk, sbs.at[n], sbr.at[n], sib).wait_send()
        for h in (0, 1):
            blk = tgt.at[z, c, h]
            rc(blk, blk, sbs.at[h], sbr.at[h], sib).wait_send()

    stages = (gather_in, gather_mid, gather_on, work, reduce_on, reduce_b, reduce_a)

    def flow(p):
        for n, (i, ch) in enumerate(ORDER):
            stages[i](p, ch)
            if p == 0 and n in RING_AT:
                ring_some(1)
            if p == 0 and n == 19:
                count_chosen()

    lane = lax.broadcasted_iota(jnp.int32, (MK, NS * MK), 1)
    sub = lax.broadcasted_iota(jnp.int32, (MK, NS * MK), 0)

    def count_chosen():
        rows = [dis[j].astype(F32) for j in range(NEG)] + [jnp.zeros((16 - NEG, MK), F32)]
        dis_f = jnp.concatenate(rows, axis=0).T
        lane_f = lane.astype(F32)
        times = jnp.where(dis_f[:, 0:1] == lane_f, 1.0, 0.0)
        for j in range(1, NEG):
            times = times + jnp.where(dis_f[:, j : j + 1] == lane_f, 1.0, 0.0)
        chosen[...] = times

    put_out(0, dot(disp_b, hid[...]))
    pl.semaphore_wait(barrier, NS - 1 + 6)
    send_out(0)
    gate_row = jnp.sum(
        own_row[0] * gate[0:1, :] + own_row[1] * gate[1:2, :], axis=1, keepdims=True
    )
    disp_t = disp.T.astype(BF)
    spread = jnp.where(lax.broadcasted_iota(jnp.int32, (FR, MK), 0) == pos[0:1, :], 1.0, 0.0)
    spread_b = spread.astype(BF)
    pick_b = spread.T.astype(BF)
    mrow_t = dot(disp_b, spread_b)
    for cp in loads[5:]:
        cp.wait()
    picked_hidden = dot(pick_b, hid[...])
    win[...] = wint[...].T
    woutt[...] = wout[...].T
    flow(0)
    ring_some(17)

    own = jnp.where(lane == sub + s * MK, 1.0, 0.0)
    count = chosen[...] + own
    shared_done()
    norms = []
    for q in range(NZ):
        v = tgt[q].reshape(2 * MK, D).astype(F32)
        n2 = jnp.sum(v * v, axis=1, keepdims=True)
        norms.append(jnp.broadcast_to(n2, (2 * MK, 128)).T[0:1, :])
    t_inv = 1.0 / jnp.sqrt(jnp.concatenate(norms, axis=1) + EPS)

    eout = returned(0)
    coef = (mrow_t * gate_row).T
    c_hi, c_lo = pieces(coef)
    mixed = picked_hidden + (dot(c_hi, eout) + dot(c_lo, eout))
    ctx_b = mixed.astype(BF)
    ctx = ctx_b.astype(F32)
    c_inv = 1.0 / jnp.sqrt(jnp.sum(ctx * ctx, axis=1, keepdims=True) + EPS)
    everyone = tgt[...].reshape(NS * MK, D)
    logits = dot_nt(ctx_b, everyone) * (c_inv * (1.0 / SHARP)) * t_inv
    log_total = jnp.log(jnp.sum(count * jnp.exp(logits), axis=1, keepdims=True))
    loss = log_total - jnp.sum(own * logits, axis=1, keepdims=True)
    lossv[:, :MK] = jnp.broadcast_to(loss, (MK, 128)).T[0:1, :]
    share = count * jnp.exp(logits - log_total)
    coef = (share - own) * (SCALE / SHARP) * t_inv
    c_hi, c_lo = pieces(coef)
    grad_unit = dot(c_hi, everyone) + dot(c_lo, everyone)
    ctx_unit = ctx * c_inv
    along = jnp.sum(grad_unit * ctx_unit, axis=1, keepdims=True)
    grad_ctx = (grad_unit - along * ctx_unit) * c_inv
    g_hi, g_lo = pieces(grad_ctx)
    g_two = jnp.concatenate([g_hi, g_lo], axis=0)

    mrow_b = mrow_t.astype(BF)
    grad_rows = dot(jnp.concatenate([mrow_b, mrow_b], axis=1), g_two) * gate_row
    put_out(1, grad_rows)
    send_out(1)
    q_two = dot_nt(eout, g_two)
    q_row = jnp.sum(mrow_t * (q_two[:, :MK] + q_two[:, MK:]), axis=1, keepdims=True)
    for t in (0, 1):
        ggv[t : t + 1, :] = jnp.sum(own_row[t] * q_row, axis=0, keepdims=True)
    grad_mixed = dot(jnp.concatenate([spread_b, spread_b], axis=1), g_two)
    outs = [
        pltpu.make_async_copy(lossv.at[:, pl.ds(0, 128)], loss_ref, osem.at[0]),
        pltpu.make_async_copy(ggv, gg_ref, osem.at[1]),
        pltpu.make_async_copy(dwov, dwo_ref, osem.at[2]),
        pltpu.make_async_copy(dwiv, dwi_ref, osem.at[3]),
        pltpu.make_async_copy(ghv, gh_ref, osem.at[4]),
    ]
    outs[0].start()
    outs[1].start()
    flow(1)

    grads = grp[1].reshape(16 * ROWS, D)
    for n in range(5):
        dwov[:, 256 * n : 256 * n + 256] = dot(act_t[...], grads[:, 256 * n : 256 * n + 256]).astype(BF)
    outs[2].start()
    rows = grp[0].reshape(16 * ROWS, D)
    for n in range(5):
        dwiv[:, 256 * n : 256 * n + 256] = dot(gpre_t[...], rows[:, 256 * n : 256 * n + 256]).astype(BF)
    outs[3].start()
    ghv[...] = (grad_mixed + dot(disp_t, returned(1))).astype(BF)
    outs[4].start()
    ring_sends_done()
    sends_done(0)
    sends_done(1)
    for cp in outs:
        cp.wait()


def local(
    hidden, gate_probs, expert_ids, slot_ids, mask_pos, distractors, targets, weight_in, weight_out
):
    dma = pltpu.SemaphoreType.DMA
    vm = pltpu.VMEM
    hbm = pl.BlockSpec(memory_space=pl.ANY)
    outs = pl.pallas_call(
        kernel,
        out_shape=(
            jax.ShapeDtypeStruct((1, 128), F32),
            jax.ShapeDtypeStruct((2, FR), F32),
            jax.ShapeDtypeStruct((FR, D), BF),
            jax.ShapeDtypeStruct((HID, D), BF),
            jax.ShapeDtypeStruct((HID, D), BF),
        ),
        in_specs=[hbm] * 9,
        out_specs=(hbm,) * 5,
        scratch_shapes=[
            vm((FR, D), BF),
            vm((2, FR), F32),
            vm((2, FR), jnp.int32),
            vm((2, FR), jnp.int32),
            vm((1, MK), jnp.int32),
            vm((NEG, 1, MK), jnp.int32),
            vm((D, HID), BF),
            vm((HID, D), BF),
            vm((HID, D), BF),
            vm((D, HID), BF),
            vm((NZ, 2, 2, 32, D), BF),
            vm((2, NS, 2, D), BF),
            vm((2, NS, 2, D), BF),
            vm((2, CHUNKS, 4, 4, 16, D), BF),
            vm((2, CHUNKS, 4, 4, 16, D), BF),
            vm((2, CHUNKS, 3, 4, 16, D), BF),
            vm((2, CHUNKS, 4, 16, D), BF),
            vm((2, CHUNKS, 3, 16, D), BF),
            vm((2, NS, 2, D), BF),
            vm((2, NS, 2, D), BF),
            vm((HID, 16 * ROWS), BF),
            vm((16 * ROWS, HID), F32),
            vm((HID, 16 * ROWS), BF),
            vm((MK, NS * MK), F32),
            vm((1, 128), F32),
            vm((2, FR), F32),
            vm((FR, D), BF),
            vm((HID, D), BF),
            vm((HID, D), BF),
            dma((10,)),
            dma((5,)),
            dma((2, CHUNKS)),
            dma((2, CHUNKS)),
            dma((2, CHUNKS, 3)),
            dma((2, CHUNKS, 3)),
            dma((2, CHUNKS, 3)),
            dma((2, CHUNKS, 3)),
            dma((2, CHUNKS, 3)),
            dma((2, CHUNKS, 3)),
            dma((2, CHUNKS, 3)),
            dma((2, CHUNKS, 3)),
            dma((2, CHUNKS)),
            dma((2, CHUNKS)),
            dma((2, 15)),
            dma((2, 15)),
            dma((32,)),
            dma((32,)),
        ],
        compiler_params=pltpu.CompilerParams(
            collective_id=0, has_side_effects=True, vmem_limit_bytes=56 * 2**20
        ),
        cost_estimate=pl.CostEstimate(
            flops=6_000_000_000, bytes_accessed=8_000_000, transcendentals=1_000_000
        ),
        name="experts",
    )(
        hidden[0], gate_probs[0], expert_ids[0], slot_ids[0], mask_pos, jnp.swapaxes(distractors, 0, 1),
        targets[0], weight_in[0].T, weight_out[0],
    )
    loss, gate_grad, grad_hidden, grad_in, grad_out = outs
    return (loss[:, :MK], gate_grad[None], grad_hidden[None], grad_in.T[None], grad_out[None])


def solution(mesh):
    return jax.shard_map(
        local,
        mesh=mesh,
        in_specs=(
            P("dp", "seq", None),
            P("dp", None, "seq"),
            P("dp", None, "seq"),
            P("dp", None, "seq"),
            P("dp", "seq"),
            P("dp", None, "seq"),
            P("dp", "seq", None),
            P("seq", None, "dp"),
            P("seq", "dp", None),
        ),
        out_specs=(
            P("dp", "seq"),
            P("dp", None, "seq"),
            P("dp", "seq", None),
            P("seq", None, "dp"),
            P("seq", "dp", None),
        ),
        check_vma=False,
    )
```

```python
import jax
import jax.numpy as jnp
from jax import lax
from jax.experimental import pallas as pl
from jax.experimental.pallas import tpu as pltpu
from jax.sharding import PartitionSpec as P

MESH = pl.DeviceIdType.MESH
BF = jnp.bfloat16
F32 = jnp.float32
NZ = 16
NS = 32
CHUNKS = 4
D = 1280
HID = 320
ROWS = 64
FR = 128
MK = 64
NEG = 10
EPS = 1e-06
SHARP = 0.1
SCALE = 64.0
ORDER = [
    (0, 0), (0, 1), (1, 0), (0, 2), (1, 1), (2, 0), (0, 3), (1, 2), (2, 1), (1, 3), (2, 2), (3, 0),
    (2, 3), (3, 1), (3, 2), (3, 3), (4, 0), (4, 1), (4, 2), (4, 3), (5, 0), (5, 1), (5, 2), (5, 3),
    (6, 0), (6, 1), (6, 2), (6, 3),
]
RING_AT = (2, 4, 6, 8, 9, 10, 11, 12, 13, 14, 15, 17, 19, 21, 23)
DZ = [0] + [(h + 1) // 2 if h % 2 else NZ - h // 2 for h in range(1, NZ)]


def dot(a, b):
    return jnp.dot(a, b, preferred_element_type=F32)


def dot_nt(a, b):
    return lax.dot_general(a, b, (((1,), (1,)), ((), ())), preferred_element_type=F32)


def pieces(v):
    hi = v.astype(BF)
    lo = (v - hi.astype(F32)).astype(BF)
    return hi, lo


def gelu_parts(x):
    k = 0.7978845608028654
    x2 = x * x
    t = jnp.tanh(k * (x + 0.044715 * (x2 * x)))
    half = 0.5 * (1.0 + t)
    slope = half + 0.5 * x * (1.0 - t * t) * (k * (1.0 + (3 * 0.044715) * x2))
    return x * half, slope


def kernel(
    hid_ref, gate_ref, exp_ref, slot_ref, pos_ref, dis_ref, tgt_ref, win_ref, wout_ref,
    loss_ref, gg_ref, gh_ref, dwi_ref, dwo_ref,
    hid, gate, exps, slots, pos, dis, win, wout, wint, woutt,
    tgt, out, inn, grp, part, rsb, acc, rsa, rout, ret,
    act_t, slope, gpre_t, chosen, lossv, ggv, ghv, dwiv, dwov,
    lsem, osem,
    ds, dr, gas, gar, gbs, gbr, bs, br, as_, ar, ts, tr,
    rgs, rgr, sbs, sbr,
):
    dp, s = lax.axis_index("dp"), lax.axis_index("seq")
    z, c = s // 2, s % 2
    y, x = dp // 4, dp % 4
    a = x + c * (y - x)
    b = y + c * (x - y)

    def dpi(aa, bb):
        return aa * (1 + 3 * c) + bb * (4 - 3 * c)

    apeer = {d: (dpi((a + d) % 4, b), s) for d in (1, 2, 3)}
    bpeer = {d: (dpi(a, (b + d) % 4), s) for d in (1, 2, 3)}

    def zpeer(k):
        return (dp, ((z + NZ - DZ[k // 2]) % NZ) * 2 + (c + k % 2) % 2)

    def zback(k):
        return (dp, ((z + DZ[k // 2]) % NZ) * 2 + (c + k % 2) % 2)

    zup = (dp, ((z + 1) % NZ) * 2 + c)
    zdn = (dp, ((z + NZ - 1) % NZ) * 2 + c)
    sib = (dp, z * 2 + 1 - c)

    def rc(src, dst, ssem, rsem, dev):
        return pltpu.make_async_remote_copy(
            src_ref=src, dst_ref=dst, send_sem=ssem, recv_sem=rsem, device_id=dev, device_id_type=MESH
        )

    loads = [
        (hid_ref, hid), (gate_ref, gate), (exp_ref, exps), (slot_ref, slots), (pos_ref, pos),
        (dis_ref, dis), (win_ref, wint), (wout_ref, wout),
    ]
    loads = [pltpu.make_async_copy(p, q, lsem.at[i]) for i, (p, q) in enumerate(loads)]
    tloads = [
        pltpu.make_async_copy(tgt_ref.at[pl.ds(32 * h, 32)], tgt.at[z, c, h], lsem.at[len(loads) + h])
        for h in (0, 1)
    ]
    for cp in loads + tloads:
        cp.start()
    barrier = pltpu.get_barrier_semaphore()
    for k in range(1, NS):
        pl.semaphore_signal(barrier, inc=1, device_id=zpeer(k), device_id_type=MESH)
    for d in (1, 2, 3):
        pl.semaphore_signal(barrier, inc=1, device_id=apeer[d], device_id_type=MESH)
        pl.semaphore_signal(barrier, inc=1, device_id=bpeer[d], device_id_type=MESH)

    for cp in loads[:5]:
        cp.wait()

    row = lax.broadcasted_iota(jnp.int32, (ROWS, FR), 0)
    kk = row >> 1
    hh = kk >> 1
    dz = jnp.where((hh & 1) == 1, (hh + 1) >> 1, (NZ - (hh >> 1)) & (NZ - 1))
    want = (((z + NZ - dz) & (NZ - 1)) << 1) + ((c + (kk & 1)) & 1)
    cap = row & 1
    own_row = [
        jnp.where((exps[t : t + 1, :] == want) & (slots[t : t + 1, :] == cap), 1.0, 0.0) for t in (0, 1)
    ]
    disp = own_row[0] + own_row[1]
    disp_b = disp.astype(BF)

    def put_out(p, rows):
        for k in range(NS):
            out[p, k] = rows[2 * k : 2 * k + 2].astype(BF)

    def send_out(p):
        for k in range(1, NS):
            rc(out.at[p, k], inn.at[p, k], ds.at[p, k // 8], dr.at[p, k // 8], zpeer(k)).start()
        inn[p, 0] = out[p, 0]

    def span(ch):
        return pl.ds(8 * ch, 8) if ch else pl.ds(1, 7)

    def gather_in(p, ch):
        rc(out.at[p, span(ch)], inn.at[p, span(ch)], ds.at[p, ch], dr.at[p, ch], zup).wait_recv()
        rows = inn[p, 8 * ch : 8 * ch + 8].astype(F32).reshape(16, D).astype(BF)
        grp[p, ch, b, a] = rows
        blk = grp.at[p, ch, b, a]
        for d in (1, 2, 3):
            rc(blk, blk, gas.at[p, ch, d - 1], gar.at[p, ch, d - 1], apeer[d]).start()

    def gather_mid(p, ch):
        for d in (1, 2, 3):
            blk = grp.at[p, ch, b, (a + 4 - d) % 4]
            rc(blk, blk, gas.at[p, ch, d - 1], gar.at[p, ch, d - 1], apeer[d]).wait_recv()
        for slot in (0, 1):
            b_copy(p, ch, slot).start()

    def fore(ch):
        return 1 if ch % 2 == 0 else 3

    def b_copy(p, ch, slot):
        g = fore(ch)
        blk = grp.at[p, ch, (b + 4 - g) % 4] if slot == 2 else grp.at[p, ch, b]
        dev = bpeer[4 - g] if slot == 1 else bpeer[g]
        return rc(blk, blk, gbs.at[p, ch, slot], gbr.at[p, ch, slot], dev)

    def b_wait(p, ch, slot):
        g = fore(ch)
        blk = grp.at[p, ch, (b + (4 - g, g, 2)[slot]) % 4]
        rc(blk, blk, gbs.at[p, ch, slot], gbr.at[p, ch, slot], bpeer[g]).wait_recv()

    def gather_on(p, ch):
        b_wait(p, ch, 0)
        b_copy(p, ch, 2).start()

    def sum_copy(p, ch, slot):
        g = fore(ch)
        blk = part.at[p, ch, (b + (2, 4 - g, g)[slot]) % 4]
        dev = bpeer[4 - g] if slot == 1 else bpeer[g]
        return rc(blk, rsb.at[p, ch, slot], bs.at[p, ch, slot], br.at[p, ch, slot], dev)

    def work(p, ch):
        b_wait(p, ch, 1)
        b_wait(p, ch, 2)
        rows = grp[p, ch].reshape(256, D)
        if p == 0:
            act, slp = gelu_parts(dot(rows, win[...]))
            act = act.astype(BF)
            part[p, ch] = dot(act, wout[...]).astype(BF).reshape(4, 4, 16, D)
        else:
            grad_pre = (dot(rows, woutt[...]) * slope[pl.ds(256 * ch, 256), :]).astype(BF)
            part[p, ch] = dot(grad_pre, wint[...]).astype(BF).reshape(4, 4, 16, D)
        sum_copy(p, ch, 0).start()
        sum_copy(p, ch, 1).start()
        if p == 0:
            slope[pl.ds(256 * ch, 256), :] = slp
            act_t[:, 256 * ch : 256 * ch + 256] = act.T
        else:
            gpre_t[:, 256 * ch : 256 * ch + 256] = grad_pre.T

    def reduce_on(p, ch):
        nxt = (b + fore(ch)) % 4
        sum_copy(p, ch, 0).wait_recv()
        part[p, ch, nxt] = (part[p, ch, nxt].astype(F32) + rsb[p, ch, 0].astype(F32)).astype(BF)
        sum_copy(p, ch, 2).start()

    def reduce_b(p, ch):
        sum_copy(p, ch, 1).wait_recv()
        sum_copy(p, ch, 2).wait_recv()
        total = part[p, ch, b].astype(F32) + (rsb[p, ch, 1].astype(F32) + rsb[p, ch, 2].astype(F32))
        acc[p, ch] = total.astype(BF)
        for d in (1, 2, 3):
            rc(
                acc.at[p, ch, (a + d) % 4], rsa.at[p, ch, d - 1], as_.at[p, ch, d - 1], ar.at[p, ch, d - 1],
                apeer[d],
            ).start()

    def reduce_a(p, ch):
        for d in (1, 2, 3):
            rc(
                acc.at[p, ch, (a + d) % 4], rsa.at[p, ch, d - 1], as_.at[p, ch, d - 1], ar.at[p, ch, d - 1],
                apeer[d],
            ).wait_recv()
        total = (acc[p, ch, a].astype(F32) + rsa[p, ch, 0].astype(F32)) + (
            rsa[p, ch, 1].astype(F32) + rsa[p, ch, 2].astype(F32)
        )
        rout[p, 8 * ch : 8 * ch + 8] = total.reshape(8, 2, D).astype(BF)
        for k in range(8 * ch, 8 * ch + 8):
            if k:
                rc(rout.at[p, k], ret.at[p, k], ts.at[p, ch], tr.at[p, ch], zback(k)).start()
        if ch == 0:
            ret[p, 0] = rout[p, 0]

    def returned(p):
        for ch in range(CHUNKS):
            rc(rout.at[p, span(ch)], ret.at[p, span(ch)], ts.at[p, ch], tr.at[p, ch], zup).wait_recv()
        return ret[p].astype(F32).reshape(ROWS, D).astype(BF)

    def sends_done(p):
        for ch in range(CHUNKS):
            rc(out.at[p, span(ch)], inn.at[p, span(ch)], ds.at[p, ch], dr.at[p, ch], zup).wait_send()
            rc(rout.at[p, span(ch)], ret.at[p, span(ch)], ts.at[p, ch], tr.at[p, ch], zup).wait_send()
            for d in (1, 2, 3):
                blk = grp.at[p, ch, b, a]
                rc(blk, blk, gas.at[p, ch, d - 1], gar.at[p, ch, d - 1], apeer[d]).wait_send()
                b_copy(p, ch, d - 1).wait_send()
                sum_copy(p, ch, d - 1).wait_send()
                rc(
                    acc.at[p, ch, (a + d) % 4], rsa.at[p, ch, d - 1], as_.at[p, ch, d - 1],
                    ar.at[p, ch, d - 1], apeer[d],
                ).wait_send()

    def ring_at(u):
        step, half = u // 2, u % 2
        up_half = half if u < 14 else 0
        dn_half = half if u < 14 else 1
        return step, up_half, dn_half

    def ring_copy(u, way):
        step, up_half, dn_half = ring_at(u)
        if way == 0:
            blk = tgt.at[(z + NZ - step) % NZ, c, up_half]
            return rc(blk, blk, rgs.at[0, u], rgr.at[0, u], zup)
        blk = tgt.at[(z + step) % NZ, c, dn_half]
        return rc(blk, blk, rgs.at[1, u], rgr.at[1, u], zdn)

    def ring_got(u, way):
        step, up_half, dn_half = ring_at(u)
        if way == 0:
            return tgt.at[(z + NZ - 1 - step) % NZ, c, up_half]
        return tgt.at[(z + 1 + step) % NZ, c, dn_half]

    def ring_take(u):
        for way in (0, 1):
            blk = ring_got(u, way)
            rc(blk, blk, rgs.at[way, u], rgr.at[way, u], zup).wait_recv()
            n = 2 + 2 * u + way
            rc(blk, blk, sbs.at[n], sbr.at[n], sib).start()

    def ring_step(u):
        if u == 0:
            for h in (0, 1):
                tloads[h].wait()
                blk = tgt.at[z, c, h]
                rc(blk, blk, sbs.at[h], sbr.at[h], sib).start()
        if 2 <= u != 15:
            ring_take(u - 2)
        if u == 14:
            ring_take(13)
        if u < 15:
            ring_copy(u, 0).start()
            ring_copy(u, 1).start()

    ring_next = [0]

    def ring_some(n):
        for _ in range(n):
            if ring_next[0] < 17:
                ring_step(ring_next[0])
                ring_next[0] += 1

    def shared_done():
        for h in (0, 1):
            blk = tgt.at[z, 1 - c, h]
            rc(blk, blk, sbs.at[h], sbr.at[h], sib).wait_recv()
        for u in range(15):
            step, up_half, dn_half = ring_at(u)
            for way in (0, 1):
                pos_z = (z + NZ - 1 - step) % NZ if way == 0 else (z + 1 + step) % NZ
                blk = tgt.at[pos_z, 1 - c, up_half if way == 0 else dn_half]
                n = 2 + 2 * u + way
                rc(blk, blk, sbs.at[n], sbr.at[n], sib).wait_recv()

    def ring_sends_done():
        for u in range(15):
            for way in (0, 1):
                ring_copy(u, way).wait_send()
                blk = ring_got(u, way)
                n = 2 + 2 * u + way
                rc(blk, blk, sbs.at[n], sbr.at[n], sib).wait_send()
        for h in (0, 1):
            blk = tgt.at[z, c, h]
            rc(blk, blk, sbs.at[h], sbr.at[h], sib).wait_send()

    stages = (gather_in, gather_mid, gather_on, work, reduce_on, reduce_b, reduce_a)

    def flow(p):
        for n, (i, ch) in enumerate(ORDER):
            stages[i](p, ch)
            if p == 0 and n in RING_AT:
                ring_some(1)
            if p == 0 and n == 19:
                count_chosen()

    lane = lax.broadcasted_iota(jnp.int32, (MK, NS * MK), 1)
    sub = lax.broadcasted_iota(jnp.int32, (MK, NS * MK), 0)

    def count_chosen():
        rows = [dis[j].astype(F32) for j in range(NEG)] + [jnp.zeros((16 - NEG, MK), F32)]
        dis_f = jnp.concatenate(rows, axis=0).T
        lane_f = lane.astype(F32)
        times = jnp.where(dis_f[:, 0:1] == lane_f, 1.0, 0.0)
        for j in range(1, NEG):
            times = times + jnp.where(dis_f[:, j : j + 1] == lane_f, 1.0, 0.0)
        chosen[...] = times

    put_out(0, dot(disp_b, hid[...]))
    pl.semaphore_wait(barrier, NS - 1 + 6)
    send_out(0)
    gate_row = jnp.sum(
        own_row[0] * gate[0:1, :] + own_row[1] * gate[1:2, :], axis=1, keepdims=True
    )
    disp_t = disp.T.astype(BF)
    spread = jnp.where(lax.broadcasted_iota(jnp.int32, (FR, MK), 0) == pos[0:1, :], 1.0, 0.0)
    spread_b = spread.astype(BF)
    pick_b = spread.T.astype(BF)
    mrow_t = dot(disp_b, spread_b)
    for cp in loads[5:]:
        cp.wait()
    picked_hidden = dot(pick_b, hid[...])
    win[...] = wint[...].T
    woutt[...] = wout[...].T
    flow(0)
    ring_some(17)

    own = jnp.where(lane == sub + s * MK, 1.0, 0.0)
    count = chosen[...] + own
    shared_done()
    norms = []
    for q in range(NZ):
        v = tgt[q].reshape(2 * MK, D).astype(F32)
        n2 = jnp.sum(v * v, axis=1, keepdims=True)
        norms.append(jnp.broadcast_to(n2, (2 * MK, 128)).T[0:1, :])
    t_inv = 1.0 / jnp.sqrt(jnp.concatenate(norms, axis=1) + EPS)

    eout = returned(0)
    coef = (mrow_t * gate_row).T
    c_hi, c_lo = pieces(coef)
    mixed = picked_hidden + (dot(c_hi, eout) + dot(c_lo, eout))
    ctx_b = mixed.astype(BF)
    ctx = ctx_b.astype(F32)
    c_inv = 1.0 / jnp.sqrt(jnp.sum(ctx * ctx, axis=1, keepdims=True) + EPS)
    everyone = tgt[...].reshape(NS * MK, D)
    logits = dot_nt(ctx_b, everyone) * (c_inv * (1.0 / SHARP)) * t_inv
    log_total = jnp.log(jnp.sum(count * jnp.exp(logits), axis=1, keepdims=True))
    loss = log_total - jnp.sum(own * logits, axis=1, keepdims=True)
    lossv[:, :MK] = jnp.broadcast_to(loss, (MK, 128)).T[0:1, :]
    share = count * jnp.exp(logits - log_total)
    coef = (share - own) * (SCALE / SHARP) * t_inv
    c_hi, c_lo = pieces(coef)
    grad_unit = dot(c_hi, everyone) + dot(c_lo, everyone)
    ctx_unit = ctx * c_inv
    along = jnp.sum(grad_unit * ctx_unit, axis=1, keepdims=True)
    grad_ctx = (grad_unit - along * ctx_unit) * c_inv
    g_hi, g_lo = pieces(grad_ctx)
    g_two = jnp.concatenate([g_hi, g_lo], axis=0)

    mrow_b = mrow_t.astype(BF)
    grad_rows = dot(jnp.concatenate([mrow_b, mrow_b], axis=1), g_two) * gate_row
    put_out(1, grad_rows)
    send_out(1)
    q_two = dot_nt(eout, g_two)
    q_row = jnp.sum(mrow_t * (q_two[:, :MK] + q_two[:, MK:]), axis=1, keepdims=True)
    for t in (0, 1):
        ggv[t : t + 1, :] = jnp.sum(own_row[t] * q_row, axis=0, keepdims=True)
    grad_mixed = dot(jnp.concatenate([spread_b, spread_b], axis=1), g_two)
    outs = [
        pltpu.make_async_copy(lossv.at[:, pl.ds(0, 128)], loss_ref, osem.at[0]),
        pltpu.make_async_copy(ggv, gg_ref, osem.at[1]),
        pltpu.make_async_copy(dwov, dwo_ref, osem.at[2]),
        pltpu.make_async_copy(dwiv, dwi_ref, osem.at[3]),
        pltpu.make_async_copy(ghv, gh_ref, osem.at[4]),
    ]
    outs[0].start()
    outs[1].start()
    flow(1)

    grads = grp[1].reshape(16 * ROWS, D)
    for n in range(5):
        dwov[:, 256 * n : 256 * n + 256] = dot(act_t[...], grads[:, 256 * n : 256 * n + 256]).astype(BF)
    outs[2].start()
    rows = grp[0].reshape(16 * ROWS, D)
    for n in range(5):
        dwiv[:, 256 * n : 256 * n + 256] = dot(gpre_t[...], rows[:, 256 * n : 256 * n + 256]).astype(BF)
    outs[3].start()
    ghv[...] = (grad_mixed + dot(disp_t, returned(1))).astype(BF)
    outs[4].start()
    ring_sends_done()
    sends_done(0)
    sends_done(1)
    for cp in outs:
        cp.wait()


def local(
    hidden, gate_probs, expert_ids, slot_ids, mask_pos, distractors, targets, weight_in, weight_out
):
    dma = pltpu.SemaphoreType.DMA
    vm = pltpu.VMEM
    hbm = pl.BlockSpec(memory_space=pl.ANY)
    outs = pl.pallas_call(
        kernel,
        out_shape=(
            jax.ShapeDtypeStruct((1, 128), F32),
            jax.ShapeDtypeStruct((2, FR), F32),
            jax.ShapeDtypeStruct((FR, D), BF),
            jax.ShapeDtypeStruct((HID, D), BF),
            jax.ShapeDtypeStruct((HID, D), BF),
        ),
        in_specs=[hbm] * 9,
        out_specs=(hbm,) * 5,
        scratch_shapes=[
            vm((FR, D), BF),
            vm((2, FR), F32),
            vm((2, FR), jnp.int32),
            vm((2, FR), jnp.int32),
            vm((1, MK), jnp.int32),
            vm((NEG, 1, MK), jnp.int32),
            vm((D, HID), BF),
            vm((HID, D), BF),
            vm((HID, D), BF),
            vm((D, HID), BF),
            vm((NZ, 2, 2, 32, D), BF),
            vm((2, NS, 2, D), BF),
            vm((2, NS, 2, D), BF),
            vm((2, CHUNKS, 4, 4, 16, D), BF),
            vm((2, CHUNKS, 4, 4, 16, D), BF),
            vm((2, CHUNKS, 3, 4, 16, D), BF),
            vm((2, CHUNKS, 4, 16, D), BF),
            vm((2, CHUNKS, 3, 16, D), BF),
            vm((2, NS, 2, D), BF),
            vm((2, NS, 2, D), BF),
            vm((HID, 16 * ROWS), BF),
            vm((16 * ROWS, HID), F32),
            vm((HID, 16 * ROWS), BF),
            vm((MK, NS * MK), F32),
            vm((1, 128), F32),
            vm((2, FR), F32),
            vm((FR, D), BF),
            vm((HID, D), BF),
            vm((HID, D), BF),
            dma((10,)),
            dma((5,)),
            dma((2, CHUNKS)),
            dma((2, CHUNKS)),
            dma((2, CHUNKS, 3)),
            dma((2, CHUNKS, 3)),
            dma((2, CHUNKS, 3)),
            dma((2, CHUNKS, 3)),
            dma((2, CHUNKS, 3)),
            dma((2, CHUNKS, 3)),
            dma((2, CHUNKS, 3)),
            dma((2, CHUNKS, 3)),
            dma((2, CHUNKS)),
            dma((2, CHUNKS)),
            dma((2, 15)),
            dma((2, 15)),
            dma((32,)),
            dma((32,)),
        ],
        compiler_params=pltpu.CompilerParams(
            collective_id=0, has_side_effects=True, vmem_limit_bytes=56 * 2**20
        ),
        cost_estimate=pl.CostEstimate(
            flops=6_000_000_000, bytes_accessed=8_000_000, transcendentals=1_000_000
        ),
        name="experts",
    )(
        hidden[0], gate_probs[0], expert_ids[0], slot_ids[0], mask_pos, jnp.swapaxes(distractors, 0, 1),
        targets[0], weight_in[0].T, weight_out[0],
    )
    loss, gate_grad, grad_hidden, grad_in, grad_out = outs
    return (loss[:, :MK], gate_grad[None], grad_hidden[None], grad_in.T[None], grad_out[None])


def solution(mesh):
    return jax.shard_map(
        local,
        mesh=mesh,
        in_specs=(
            P("dp", "seq", None),
            P("dp", None, "seq"),
            P("dp", None, "seq"),
            P("dp", None, "seq"),
            P("dp", "seq"),
            P("dp", None, "seq"),
            P("dp", "seq", None),
            P("seq", None, "dp"),
            P("seq", "dp", None),
        ),
        out_specs=(
            P("dp", "seq"),
            P("dp", None, "seq"),
            P("dp", "seq", None),
            P("seq", None, "dp"),
            P("seq", "dp", None),
        ),
        check_vma=False,
    )
```
